128 devices in a mesh: node: 16 (over z, y), local: 8 (over x, core).
Axes of the slice: x: 4, y: 4, z: 4, core: 2. Of those that a mesh axis runs over, the one named last changes fastest.
Arguments:
- tokens: bfloat16 [8192, 3584], P(('node', 'local')), may hold values from -6 to 6
- expert_ids: int32 [8192, 8], P(('node', 'local')), may hold values from 0 to 127, as said below
- gate_weights: bfloat16 [8192, 8], P(('node', 'local')), may hold values from 0.099609375 to 1
- expert_gate: bfloat16 [128, 3584, 1024], P(('node', 'local')), may hold values from -0.09375 to 0.09375
- expert_up: bfloat16 [128, 3584, 1024], P(('node', 'local')), may hold values from -0.09375 to 0.09375
- expert_down: bfloat16 [128, 1024, 3584], P(('node', 'local')), may hold values from -0.1875 to 0.1875
- shared_gate: bfloat16 [3584, 1024], P(None, 'local'), may hold values from -0.09375 to 0.09375
- shared_up: bfloat16 [3584, 1024], P(None, 'local'), may hold values from -0.09375 to 0.09375
- shared_down: bfloat16 [1024, 3584], P('local'), may hold values from -0.1875 to 0.1875
Outputs:
- mixed: bfloat16 [8192, 3584], P(('node', 'local'))
The draws below stay inside these ranges and needn't reach their ends.
Inputs may be any that keep to these rules, and one draw needn't show every extreme that they name: `expert_ids`: expert e lives on node e // 8. Entries 2j and 2j + 1 of a row name two different experts of one node, and the 4 nodes of a row differ. Among the 64 rows of one device, half of the nodes receive exactly 24 rows and the other half exactly 8; the rows of one device that reach one node name each expert of that node equally often, so at most 6 rows of one device name one expert, and exactly that many for the busier nodes.
All inputs are finite; a program needn't handle non-finite values.
Results may differ from the reference program's by a relative error of at most 0.013.
Values may be sent and summed in bfloat16 or wider, within the bound.
A program may use at most 128 MiB of HBM per device.

```python
import math
import jax
import jax.numpy as jnp
import numpy as np
from jax import lax

D = 3584
MOE_H = 1024
SH = 1024
TOP = 8
NODES_TOK = 4
TOK_DEV = 64
EXPERTS = 128
TOKENS = 8192
EXP_CAP = 6
N_NODE = 16
N_LOCAL = 8


def draw_expert_ids(key, part):
    key = jax.random.fold_in(key, 7)
    device_count = N_NODE * N_LOCAL
    mean_load = 4 * TOK_DEV // N_NODE
    node_quota = np.where(np.arange(N_NODE) < N_NODE // 2, 3 * mean_load // 2, mean_load // 2)
    rank_table = np.repeat(np.arange(N_NODE), node_quota).reshape(NODES_TOK, TOK_DEV).T
    node_keys, token_keys, local_keys = jax.random.split(key, 3)
    node_perm = jax.vmap(lambda subkey: jax.random.permutation(subkey, N_NODE))(jax.random.split(node_keys, device_count))
    token_perm = jax.vmap(lambda subkey: jax.random.permutation(subkey, TOK_DEV))(jax.random.split(token_keys, device_count))
    local_perm = jax.vmap(lambda subkey: jax.random.permutation(subkey, N_LOCAL))(jax.random.split(local_keys, device_count * N_NODE))
    local_perm = local_perm.reshape(device_count, N_NODE, N_LOCAL)
    slot_ranks = jnp.asarray(rank_table, jnp.int32)[token_perm]
    chosen_nodes = jax.vmap(lambda table_row, lookup: table_row[lookup])(node_perm, slot_ranks)
    matches = (chosen_nodes[..., None] == jnp.arange(N_NODE, dtype=jnp.int32)).astype(jnp.int32).sum(axis=2)
    before = jnp.cumsum(matches, axis=1) - matches
    arrival_rank = jnp.take_along_axis(before, chosen_nodes, axis=2)
    local_order = jax.vmap(lambda table_row, lookup: table_row[lookup])(local_perm, chosen_nodes)
    first_local = jnp.take_along_axis(local_order, (2 * arrival_rank % N_LOCAL)[..., None], axis=3)[..., 0]
    second_local = jnp.take_along_axis(local_order, ((2 * arrival_rank + 1) % N_LOCAL)[..., None], axis=3)[..., 0]
    expert_pairs = jnp.stack([chosen_nodes * N_LOCAL + first_local, chosen_nodes * N_LOCAL + second_local], axis=-1)
    return expert_pairs.reshape(device_count * TOK_DEV, NODES_TOK * 2).astype(jnp.int32)


def block_scale(own_key, extent, cuts, least, high):
    loudness = 1.0
    for position, parts in cuts:
        heights = jax.random.uniform(jax.random.fold_in(jax.random.fold_in(own_key, 6), position), (parts,), jnp.float32, least / len(cuts), high / len(cuts))
        loudness = loudness * jnp.repeat(jnp.exp(heights), extent[position] // parts).reshape((-1,) + (1,) * (len(extent) - 1 - position))
    return loudness


def centred(key, dims, deviation, reach, pieces=(), held_as=jnp.bfloat16):
    loudness = block_scale(key, dims, pieces, -0.22, 0.18) if pieces else 1.0
    array = jax.random.normal(key, dims, jnp.float32) * deviation * loudness
    return jnp.minimum(jnp.maximum(array, -reach), reach).astype(held_as)


def setup_inputs(seed: int = 0) -> dict:
    splits = jax.random.split(jax.random.key(seed), 10)
    return {
        "tokens": centred(splits[0], (TOKENS, D), 1.0, 6.0, ((0, 128),)),
        "expert_ids": draw_expert_ids(jax.random.fold_in(splits[9], 71), 0),
        "gate_weights": jnp.clip(jnp.exp(math.log(1.0) - 2.306499 * jax.random.uniform(splits[2], (TOKENS, TOP), jnp.float32) ** block_scale(splits[2], (TOKENS, TOP), ((0, 128),), -0.2, 0.2)), 0.099609375, 1.0).astype(jnp.bfloat16),
        "expert_gate": centred(splits[3], (EXPERTS, D, MOE_H), D ** -0.5, 0.09375, ((0, 128),)),
        "expert_up": centred(splits[4], (EXPERTS, D, MOE_H), D ** -0.5, 0.09375, ((0, 128),)),
        "expert_down": centred(splits[5], (EXPERTS, MOE_H, D), MOE_H ** -0.5, 0.1875, ((0, 128),)),
        "shared_gate": centred(splits[6], (D, SH), D ** -0.5, 0.09375, ((1, 8),)),
        "shared_up": centred(splits[7], (D, SH), D ** -0.5, 0.09375, ((1, 8),)),
        "shared_down": centred(splits[8], (SH, D), SH ** -0.5, 0.1875, ((0, 8),)),
    }


def expert_apply(inputs, gate_matrix, up_matrix, down_matrix):
    gate_part = jnp.dot(inputs, gate_matrix, preferred_element_type=jnp.float32)
    up_part = jnp.dot(inputs, up_matrix, preferred_element_type=jnp.float32)
    hidden = (jax.nn.silu(gate_part) * up_part).astype(jnp.bfloat16)
    return jnp.dot(hidden, down_matrix, preferred_element_type=jnp.float32)


def reference(tokens, expert_ids, gate_weights, expert_gate, expert_up, expert_down, shared_gate, shared_up, shared_down):
    pair_count = TOKENS * TOP
    flat_ids = expert_ids.reshape(-1)
    capacity = N_NODE * N_LOCAL * EXP_CAP

    def per_expert(expert):
        chosen = flat_ids == expert
        positions = jnp.nonzero(chosen, size=capacity, fill_value=0)[0].astype(jnp.int32)
        filled = jnp.arange(capacity, dtype=jnp.int32) < jnp.sum(chosen.astype(jnp.int32))
        inputs = tokens[positions // TOP]
        outputs = expert_apply(inputs, expert_gate[expert], expert_up[expert], expert_down[expert]).astype(jnp.bfloat16)
        return outputs, jnp.where(filled, positions, pair_count).astype(jnp.int32)

    outputs, targets = lax.map(per_expert, jnp.arange(EXPERTS, dtype=jnp.int32))
    pair_out = jnp.zeros((pair_count, D), jnp.bfloat16).at[targets.reshape(-1)].set(outputs.reshape(-1, D), mode="drop")
    pair_out = pair_out.reshape(TOKENS, NODES_TOK, 2, D).astype(jnp.float32)
    gate_pairs = gate_weights.reshape(TOKENS, NODES_TOK, 2, 1).astype(jnp.float32)
    node_partial = jnp.sum(gate_pairs * pair_out, axis=2).astype(jnp.bfloat16)
    routed = jnp.sum(node_partial.astype(jnp.float32), axis=1)
    shared_out = expert_apply(tokens, shared_gate, shared_up, shared_down)
    return (shared_out + routed).astype(jnp.bfloat16)
```

```python
import functools

import jax
import jax.numpy as jnp
from jax import lax
from jax.experimental import pallas as pl
from jax.experimental.pallas import tpu as pltpu
from jax.sharding import PartitionSpec as P

MESH = pl.DeviceIdType.MESH
BF16 = jnp.bfloat16
F32 = jnp.float32

D = 3584
H = 1024
TOP = 8
TOK = 64
NODES = 16
LOCALS = 8
GROUP = TOK * LOCALS
SLOT = 48
ROWS = NODES * SLOT
COLS = 512
CHUNKS = D // COLS
HALF = GROUP // 2
SHARE = 128
ROW_TILE = 256


def dot(a, b):
    return jnp.dot(a, b, preferred_element_type=F32)


def silu_mul(gate, up):
    return gate / (1.0 + jnp.exp(-gate)) * up


def kernel(
    tokens, ids, weights, eg, eu, ed, sg, su, sd, out,
    held, out1, in1, in2, acc_g, acc_u, hidden, wg, wu, wd, ws, wsd, acc_s, hid_s,
    pick, mix, meta, meta_all, from_sib, from_x,
    load_sem, own_sem, meta_s, meta_r, ag_s, ag_r, fw_s, fw_r, d_s, d_r, c_s, c_r, rs_s, rs_r, rx_s, rx_r,
):
    node = lax.axis_index("node")
    local = lax.axis_index("local")
    z, y, x, core = node // 4, node % 4, local // 2, local % 2
    sib = (node, 2 * x + (1 - core))

    def far(j):
        return ((z + j // 4) % 4) * 4 + (y + j % 4) % 4

    def side(k):
        return (node, 2 * ((x + k) % 4) + core)

    def mate(k):
        return (node, (local + k) % LOCALS)

    def columns(c):
        return pl.ds(pl.multiple_of(c * COLS, COLS), COLS)

    barrier = pltpu.get_barrier_semaphore()
    for j in range(1, NODES):
        pl.semaphore_signal(barrier, inc=1, device_id=(far(j), local), device_id_type=MESH)
    for k in range(1, LOCALS):
        pl.semaphore_signal(barrier, inc=1, device_id=mate(k), device_id_type=MESH)

    loads = [
        pltpu.make_async_copy(sg, ws.at[:, pl.ds(0, SHARE)], load_sem.at[0]),
        pltpu.make_async_copy(su, ws.at[:, pl.ds(SHARE, SHARE)], load_sem.at[1]),
        pltpu.make_async_copy(eg.at[0], wg, load_sem.at[2]),
        pltpu.make_async_copy(eu.at[0], wu, load_sem.at[3]),
        pltpu.make_async_copy(ed.at[0], wd, load_sem.at[4]),
        pltpu.make_async_copy(sd, wsd, load_sem.at[5]),
    ]

    def own_rows():
        return pl.ds(pl.multiple_of(x * TOK, TOK), TOK)

    def own_copy(c):
        return pltpu.make_async_copy(tokens.at[:, columns(c)], held.at[c, core, own_rows()], own_sem.at[c])

    for c in range(CHUNKS):
        own_copy(c).start()
    for load in loads:
        load.start()

    meta[...] = jnp.zeros_like(meta)
    meta[:, 0:TOP] = ids[...].astype(F32)
    meta[:, TOP : 2 * TOP] = weights[...].astype(F32)

    pl.semaphore_wait(barrier, NODES - 1 + LOCALS - 1)

    def meta_copy(k):
        return pltpu.make_async_remote_copy(
            src_ref=meta, dst_ref=meta_all.at[core * 4 + x], send_sem=meta_s.at[k], recv_sem=meta_r.at[k],
            device_id=mate(k), device_id_type=MESH,
        )

    def gather_copy(c, k):
        return pltpu.make_async_remote_copy(
            src_ref=tokens.at[:, columns(c)], dst_ref=held.at[c, core, own_rows()],
            send_sem=ag_s.at[c, k], recv_sem=ag_r.at[c, k], device_id=side(k), device_id_type=MESH,
        )

    def forward_copy(c):
        return pltpu.make_async_remote_copy(
            src_ref=held.at[c, core], dst_ref=held.at[c, core], send_sem=fw_s.at[c], recv_sem=fw_r.at[c],
            device_id=sib, device_id_type=MESH,
        )

    for k in range(1, LOCALS):
        meta_copy(k).start()

    @pl.loop(0, CHUNKS)
    def _(c):
        for k in (1, 3, 2):
            gather_copy(c, k).start()

    meta_all[core * 4 + x] = meta[...]
    acc_s[...] = jnp.zeros_like(acc_s)
    acc_g[...] = jnp.zeros_like(acc_g)
    acc_u[...] = jnp.zeros_like(acc_u)
    for k in range(1, LOCALS):
        meta_copy(k).wait()

    table = jnp.transpose(meta_all[...].reshape(GROUP, 128))
    expert = lax.broadcasted_iota(jnp.int32, (NODES, GROUP), 0) * LOCALS + local
    expert = expert.astype(F32)
    chosen = jnp.zeros((NODES, GROUP), F32)
    gain = jnp.zeros((NODES, GROUP), F32)
    for k in range(TOP):
        hit = jnp.where(table[k : k + 1] == expert, 1.0, 0.0)
        chosen = chosen + hit
        gain = gain + hit * table[TOP + k : TOP + k + 1]
    earlier = lax.broadcasted_iota(jnp.int32, (GROUP, GROUP), 0) < lax.broadcasted_iota(jnp.int32, (GROUP, GROUP), 1)
    rank = dot(chosen.astype(BF16), jnp.where(earlier, 1.0, 0.0).astype(BF16))
    rank = jnp.where(chosen > 0.5, rank, -1.0)
    place = lax.broadcasted_iota(jnp.int32, (SLOT, GROUP), 0).astype(F32)
    for n in range(NODES):
        hit = jnp.where(rank[n : n + 1] == place, 1.0, 0.0)
        pick[n * SLOT : (n + 1) * SLOT] = hit.astype(BF16)

    def rows_copy(src, dst, send, recv, c, j):
        there = far(j)
        return pltpu.make_async_remote_copy(
            src_ref=src.at[c, pl.ds(pl.multiple_of(there * SLOT, SLOT), SLOT)],
            dst_ref=dst.at[c, pl.ds(pl.multiple_of(node * SLOT, SLOT), SLOT)],
            send_sem=send.at[c, j], recv_sem=recv.at[c, j], device_id=(there, local), device_id_type=MESH,
        )

    mine = pl.ds(pl.multiple_of(node * SLOT, SLOT), SLOT)
    loads[0].wait()
    loads[1].wait()

    @pl.loop(0, CHUNKS)
    def _(c):
        for k in (1, 3, 2):
            gather_copy(c, k).wait_recv()
        own_copy(c).wait()
        forward_copy(c).start()
        forward_copy(c).wait_recv()
        block = held[c].reshape(GROUP, COLS)
        out1[c] = dot(pick[...], block).astype(BF16)
        for j in range(1, NODES):
            rows_copy(out1, in1, d_s, d_r, c, j).start()
        in1[c, mine] = out1[c, mine]
        acc_s[...] += dot(block, ws[pl.ds(pl.multiple_of(c * COLS, COLS), COLS), :])

    hid_s[...] = silu_mul(acc_s[:, :SHARE], acc_s[:, SHARE:]).astype(BF16)
    for n in range(NODES):
        hit = jnp.where(rank[n : n + 1] == place, gain[n : n + 1], 0.0)
        mix[:, n * SLOT : (n + 1) * SLOT] = jnp.transpose(hit).astype(BF16)
    for load in loads[2:]:
        load.wait()

    @pl.loop(0, CHUNKS)
    def _(c):
        for j in range(1, NODES):
            rows_copy(out1, in1, d_s, d_r, c, j).wait_recv()
        depth = pl.ds(pl.multiple_of(c * COLS, COLS), COLS)
        for m in range(0, ROWS, ROW_TILE):
            acc_g[m : m + ROW_TILE] += dot(in1[c, m : m + ROW_TILE], wg[depth, :])
            acc_u[m : m + ROW_TILE] += dot(in1[c, m : m + ROW_TILE], wu[depth, :])

    for m in range(0, ROWS, ROW_TILE):
        hidden[m : m + ROW_TILE] = silu_mul(acc_g[m : m + ROW_TILE], acc_u[m : m + ROW_TILE]).astype(BF16)

    @pl.loop(0, CHUNKS)
    def _(c):
        for j in range(1, NODES):
            rows_copy(out1, in1, d_s, d_r, c, j).wait_send()
        out1[c] = dot(hidden[...], wd[:, columns(c)]).astype(BF16)
        for j in range(1, NODES):
            rows_copy(out1, in2, c_s, c_r, c, j).start()
        in2[c, mine] = out1[c, mine]
        for k in (1, 3, 2):
            gather_copy(c, k).wait_send()
        forward_copy(c).wait_send()

    def sib_copy(c):
        return pltpu.make_async_remote_copy(
            src_ref=held.at[c, 1 - core], dst_ref=from_sib.at[c], send_sem=rs_s.at[c], recv_sem=rs_r.at[c],
            device_id=sib, device_id_type=MESH,
        )

    def reduce_copy(c, k):
        return pltpu.make_async_remote_copy(
            src_ref=held.at[c, core, pl.ds(pl.multiple_of((x + k) % 4 * TOK, TOK), TOK)], dst_ref=from_x.at[c, k],
            send_sem=rx_s.at[c, k], recv_sem=rx_r.at[c, k], device_id=side(k), device_id_type=MESH,
        )

    @pl.loop(0, CHUNKS)
    def _(c):
        for j in range(1, NODES):
            rows_copy(out1, in2, c_s, c_r, c, j).wait_recv()
        part = dot(mix[...], in2[c]) + dot(hid_s[...], wsd[:, columns(c)])
        held[c] = part.astype(BF16).reshape(2, HALF, COLS)
        sib_copy(c).start()
        sib_copy(c).wait_recv()
        held[c, core] = (held[c, core].astype(F32) + from_sib[c].astype(F32)).astype(BF16)
        for k in (1, 3, 2):
            reduce_copy(c, k).start()
        total = held[c, core, own_rows()].astype(F32)
        for k in (1, 3, 2):
            reduce_copy(c, k).wait_recv()
            total = total + from_x[c, k].astype(F32)
        out[:, columns(c)] = total.astype(BF16)

    @pl.loop(0, CHUNKS)
    def _(c):
        for j in range(1, NODES):
            rows_copy(out1, in2, c_s, c_r, c, j).wait_send()
        sib_copy(c).wait_send()
        for k in (1, 3, 2):
            reduce_copy(c, k).wait_send()


def on_device(*arrays):
    vmem = pl.BlockSpec(memory_space=pltpu.VMEM)
    hbm = pl.BlockSpec(memory_space=pl.ANY)
    dma = pltpu.SemaphoreType.DMA
    return pl.pallas_call(
        kernel,
        out_shape=jax.ShapeDtypeStruct((TOK, D), BF16),
        in_specs=[hbm, vmem, vmem] + [hbm] * 6,
        out_specs=vmem,
        scratch_shapes=[
            pltpu.VMEM((CHUNKS, 2, HALF, COLS), BF16),
            pltpu.VMEM((CHUNKS, ROWS, COLS), BF16),
            pltpu.VMEM((CHUNKS, ROWS, COLS), BF16),
            pltpu.VMEM((CHUNKS, ROWS, COLS), BF16),
            pltpu.VMEM((ROWS, H), F32),
            pltpu.VMEM((ROWS, H), F32),
            pltpu.VMEM((ROWS, H), BF16),
            pltpu.VMEM((D, H), BF16),
            pltpu.VMEM((D, H), BF16),
            pltpu.VMEM((H, D), BF16),
            pltpu.VMEM((D, 2 * SHARE), BF16),
            pltpu.VMEM((SHARE, D), BF16),
            pltpu.VMEM((GROUP, 2 * SHARE), F32),
            pltpu.VMEM((GROUP, SHARE), BF16),
            pltpu.VMEM((ROWS, GROUP), BF16),
            pltpu.VMEM((GROUP, ROWS), BF16),
            pltpu.VMEM((TOK, 128), F32),
            pltpu.VMEM((LOCALS, TOK, 128), F32),
            pltpu.VMEM((CHUNKS, HALF, COLS), BF16),
            pltpu.VMEM((CHUNKS, 4, TOK, COLS), BF16),
            dma((6,)),
            dma((CHUNKS,)),
            dma((LOCALS,)),
            dma((LOCALS,)),
            dma((CHUNKS, 4)),
            dma((CHUNKS, 4)),
            dma((CHUNKS,)),
            dma((CHUNKS,)),
            dma((CHUNKS, NODES)),
            dma((CHUNKS, NODES)),
            dma((CHUNKS, NODES)),
            dma((CHUNKS, NODES)),
            dma((CHUNKS,)),
            dma((CHUNKS,)),
            dma((CHUNKS, 4)),
            dma((CHUNKS, 4)),
        ],
        compiler_params=pltpu.CompilerParams(
            collective_id=0, has_side_effects=True, vmem_limit_bytes=63 * 2**20
        ),
        cost_estimate=pl.CostEstimate(flops=26 * 10**9, bytes_accessed=26 * 10**6, transcendentals=10**6),
        name="moe",
    )(*arrays)


def solution(mesh):
    both = ("node", "local")
    in_specs = (
        P(both, None),
        P(both, None),
        P(both, None),
        P(both, None, None),
        P(both, None, None),
        P(both, None, None),
        P(None, "local"),
        P(None, "local"),
        P("local", None),
    )
    return jax.shard_map(on_device, mesh=mesh, in_specs=in_specs, out_specs=P(both, None), check_vma=False)
```

```python
import jax
import jax.numpy as jnp
from jax import lax
from jax.experimental import pallas as pl
from jax.experimental.pallas import tpu as pltpu
from jax.sharding import PartitionSpec as P

MESH = pl.DeviceIdType.MESH
BF16 = jnp.bfloat16
F32 = jnp.float32

D = 3584
H = 1024
TOP = 8
TOK = 64
NODES = 16
LOCALS = 8
GROUP = TOK * LOCALS
PAIR = 2 * TOK
SLOT = 48
PART = 12
BAND = NODES * PART
ROWS = NODES * SLOT
SPREAD = LOCALS * BAND
COLS = 512
WIDE = COLS // 2
CHUNKS = D // COLS
ONCE = 3
DIRECT = CHUNKS - ONCE
HALF = GROUP // 2
SHARE = 128
ROW_TILE = 256
SLOTS = 3


def dot(a, b):
    return jnp.dot(a, b, preferred_element_type=F32)


def silu_mul(gate, up):
    return gate / (1.0 + jnp.exp(-gate)) * up


def count(shape, dim):
    return lax.broadcasted_iota(jnp.int32, shape, dim).astype(F32)


def quotient(values, by):
    return jnp.floor((values + 0.5) * (1.0 / by))


def ones_where(condition):
    return jnp.where(condition, 1.0, 0.0)


def kernel(
    tokens, ids, weights, eg, eu, ed, sg, su, sd, out,
    held, out1, in1, in2, ao, ai, ae, xo, xi, xe, acc_g, acc_u, hidden, hidden_a, wgu, wds, ws, wsd, acc_s, hid_s,
    pick, mix, pick_a, mix_a, spread, merge, square, work, meta, meta_all, slots_out, slots_in, from_sib, from_x,
    load_sem, gu_sem, wd_sem, own_sem, meta_s, meta_r, sm_s, sm_r, ag_s, ag_r, fw_s, fw_r,
    d_s, d_r, c_s, c_r, ad_s, ad_r, ac_s, ac_r, xd_s, xd_r, xc_s, xc_r, rs_s, rs_r, rx_s, rx_r,
):
    node = lax.axis_index("node")
    local = lax.axis_index("local")
    z, y, x, core = node // 4, node % 4, local // 2, local % 2
    sib = (node, 2 * x + (1 - core))

    def far(j):
        return ((z + j // 4) % 4) * 4 + (y + j % 4) % 4

    def side(k):
        return (node, 2 * ((x + k) % 4) + core)

    def mate(k):
        return (local + k) % LOCALS

    def block(i, size):
        return pl.ds(pl.multiple_of(i * size, size), size)

    def columns(c):
        return block(c, COLS)

    def tok_rows(i):
        return block(i, TOK)

    def remote(src, dst, send, recv, device):
        return pltpu.make_async_remote_copy(
            src_ref=src, dst_ref=dst, send_sem=send, recv_sem=recv, device_id=device, device_id_type=MESH
        )

    barrier = pltpu.get_barrier_semaphore()
    for j in range(1, NODES):
        pl.semaphore_signal(barrier, inc=1, device_id=(far(j), local), device_id_type=MESH)
    for k in range(1, LOCALS):
        pl.semaphore_signal(barrier, inc=1, device_id=(node, mate(k)), device_id_type=MESH)

    loads = [
        pltpu.make_async_copy(sg, ws.at[:, pl.ds(0, SHARE)], load_sem.at[0]),
        pltpu.make_async_copy(su, ws.at[:, pl.ds(SHARE, SHARE)], load_sem.at[1]),
        pltpu.make_async_copy(sd, wsd, load_sem.at[2]),
    ]

    def own_copy(c):
        return pltpu.make_async_copy(tokens.at[:, columns(c)], held.at[c, core, tok_rows(x)], own_sem.at[c])

    def gate_load(c, s):
        return pltpu.make_async_copy(eg.at[0, columns(c)], wgu.at[s, 0], gu_sem.at[s, 0])

    def up_load(c, s):
        return pltpu.make_async_copy(eu.at[0, columns(c)], wgu.at[s, 1], gu_sem.at[s, 1])

    def down_load(c, s):
        return pltpu.make_async_copy(ed.at[0, :, columns(c)], wds.at[s], wd_sem.at[s])

    def in_turn(q):
        return (1 - q % 2) * ONCE + q // 2

    for c in range(CHUNKS):
        own_copy(c).start()

    meta[...] = jnp.zeros_like(meta)
    meta[0:TOP, 0:TOK] = ids[...].astype(F32) + 1.0
    meta[TOP : 2 * TOP, 0:TOK] = weights[...].astype(F32)

    pl.semaphore_wait(barrier, NODES - 1 + LOCALS - 1)

    def meta_copy(k):
        return remote(meta, meta_all.at[core * 4 + x], meta_s.at[k], meta_r.at[k], (node, mate(k)))

    def gather_copy(c, k):
        return remote(tokens.at[:, columns(c)], held.at[c, core, tok_rows(x)], ag_s.at[c, k], ag_r.at[c, k], side(k))

    def forward_copy(c, k):
        mid = held.at[c, core, tok_rows((x + 4 - k) % 4)]
        return remote(tokens.at[:, columns(c)] if k == 0 else mid, mid, fw_s.at[c, k], fw_r.at[c, k], sib)

    for k in range(1, LOCALS):
        meta_copy(k).start()
    for c in range(CHUNKS):
        forward_copy(c, 0).start()

    @pl.loop(ONCE, CHUNKS)
    def _(c):
        for k in (1, 3, 2):
            gather_copy(c, k).start()

    for load in loads:
        load.start()
    for s in range(SLOTS):
        gate_load(in_turn(s), s).start()
        up_load(in_turn(s), s).start()
        down_load(s, s).start()
    meta_all[core * 4 + x] = meta[...]
    slots_out[...] = jnp.zeros_like(slots_out)
    for k in range(1, LOCALS):
        meta_copy(k).wait()

    chip_table = jnp.concatenate([meta_all[x][:, :TOK], meta_all[4 + x][:, :TOK]], axis=1)
    chip_node = quotient(chip_table[:TOP] - 1.0, LOCALS)
    node_row = count((NODES, PAIR), 0)
    chosen = jnp.zeros((NODES, PAIR), F32)
    for k in range(0, TOP, 2):
        chosen = chosen + ones_where(chip_node[k : k + 1] == node_row)
    earlier = count((PAIR, PAIR), 0) < count((PAIR, PAIR), 1)
    rank_a = dot(chosen.astype(BF16), ones_where(earlier).astype(BF16))
    rank_a = jnp.where(chosen > 0.5, rank_a, -1.0)
    place_a = count((SLOT, PAIR), 0)
    for n in range(NODES):
        pick_a[n * SLOT : (n + 1) * SLOT] = ones_where(rank_a[n : n + 1] == place_a).astype(BF16)
    notes = lax.dot_general(
        chip_table.astype(BF16), pick_a[...], (((1,), (1,)), ((), ())), preferred_element_type=F32
    )
    for n in range(NODES):
        slots_out[n, :, 0:SLOT] = notes[:, n * SLOT : (n + 1) * SLOT]

    def notes_copy(j):
        there = far(j)
        return remote(slots_out.at[there], slots_in.at[node], sm_s.at[j], sm_r.at[j], (there, local))

    def rows_copy(src, dst, send, recv, c, j):
        there = far(j)
        return remote(
            src.at[c, block(there, SLOT)], dst.at[c, block(node, SLOT)], send.at[c, j], recv.at[c, j], (there, local)
        )

    mine = block(node, SLOT)
    wide = block(core, WIDE)

    for j in range(1, NODES):
        notes_copy(j).start()
    slots_in[node] = slots_out[node]

    @pl.loop(0, ONCE)
    def _(a):
        own_copy(a).wait()
        forward_copy(a, 0).wait_recv()
        rows = jnp.concatenate([held[a, 0, tok_rows(x), wide], held[a, 1, tok_rows(x), wide]], axis=0)
        ao[a] = dot(pick_a[...], rows).astype(BF16)
        for j in range(1, NODES):
            rows_copy(ao, ai, ad_s, ad_r, a, j).start()
        ai[a, mine] = ao[a, mine]

    table = jnp.concatenate([meta_all[d][:, :TOK] for d in range(LOCALS)], axis=1)
    expert = count((NODES, GROUP), 0) * LOCALS + (local + 1).astype(F32)
    chosen = jnp.zeros((NODES, GROUP), F32)
    gain = jnp.zeros((NODES, GROUP), F32)
    for k in range(TOP):
        hit = ones_where(table[k : k + 1] == expert)
        chosen = chosen + hit
        gain = gain + hit * table[TOP + k : TOP + k + 1]

    def chip_of(t):
        device = quotient(t, TOK)
        return device - 4.0 * quotient(device, 4)

    first, then = count((GROUP, 1), 0), count((1, GROUP), 1)
    earlier = (first < then) & (chip_of(first) == chip_of(then))
    rank = dot(chosen.astype(BF16), ones_where(earlier).astype(BF16)) + chip_of(then) * PART
    rank = jnp.where(chosen > 0.5, rank, -1.0)
    place = count((SLOT, GROUP), 0)
    for n in range(NODES):
        pick[n * SLOT : (n + 1) * SLOT] = ones_where(rank[n : n + 1] == place).astype(BF16)

    acc_s[...] = jnp.zeros_like(acc_s)
    acc_g[...] = jnp.zeros_like(acc_g)
    acc_u[...] = jnp.zeros_like(acc_u)
    loads[0].wait()
    loads[1].wait()

    def gathered(c):
        for k in (1, 3, 2):
            gather_copy(c, k).wait_recv()
            forward_copy(c, k).start()
        for k in (1, 3, 2):
            forward_copy(c, k).wait_recv()
        return held[c].reshape(GROUP, COLS)

    def direct_rows(b):
        c = b + ONCE
        own_copy(c).wait()
        forward_copy(c, 0).wait_recv()
        rows = gathered(c)
        out1[b] = dot(pick[...], rows).astype(BF16)
        for j in range(1, NODES):
            rows_copy(out1, in1, d_s, d_r, b, j).start()
        in1[b, mine] = out1[b, mine]
        acc_s[...] += dot(rows, ws[columns(c), :])

    def pass_copy(a, k):
        there = mate(k)
        return remote(
            xo.at[a, block(there, BAND)], xi.at[a, block(core * 4 + x, BAND)], xd_s.at[a, k], xd_r.at[a, k], (node, there)
        )

    def pass_rows(a):
        for j in range(1, NODES):
            rows_copy(ao, ai, ad_s, ad_r, a, j).wait_recv()
        xo[a] = dot(spread[...], ai[a]).astype(BF16)
        for k in range(1, LOCALS):
            pass_copy(a, k).start()
        xi[a, block(core * 4 + x, BAND)] = xo[a, block(local, BAND)]

    direct_rows(0)

    for j in range(1, NODES):
        notes_copy(j).wait()
    slot_table = jnp.concatenate([slots_in[n][:, :SLOT] for n in range(NODES)], axis=1)
    expert = count((LOCALS, ROWS), 0) + (node * LOCALS + 1).astype(F32)
    chosen = jnp.zeros((LOCALS, ROWS), F32)
    gain_a = jnp.zeros((LOCALS, ROWS), F32)
    for k in range(TOP):
        hit = ones_where(slot_table[k : k + 1] == expert)
        chosen = chosen + hit
        gain_a = gain_a + hit * slot_table[TOP + k : TOP + k + 1]
    first, then = count((ROWS, 1), 0), count((1, ROWS), 1)
    earlier = (first < then) & (quotient(first, SLOT) == quotient(then, SLOT))
    square[...] = ones_where(earlier).astype(BF16)
    seat = dot(chosen.astype(BF16), square[...]) + quotient(then, SLOT) * PART
    seat = jnp.where(chosen > 0.5, seat, -1.0)
    place_x = count((BAND, ROWS), 0)
    for l in range(LOCALS):
        spread[l * BAND : (l + 1) * BAND] = ones_where(seat[l : l + 1] == place_x).astype(BF16)

    @pl.loop(1, DIRECT)
    def _(b):
        direct_rows(b)
        pass_rows(b - 1)

    @pl.loop(0, ONCE)
    def _(c):
        for k in (1, 3, 2):
            gather_copy(c, k).start()

    row, column = count((ROWS, 1), 0), count((1, ROWS), 1)
    by_node = quotient(row, SLOT)
    by_chip = quotient(row - by_node * SLOT, PART)
    square[...] = ones_where(row - by_node * SLOT - by_chip * PART + by_chip * BAND + by_node * PART == column).astype(BF16)
    for n in range(NODES):
        hit = jnp.where(rank[n : n + 1] == place, gain[n : n + 1], 0.0)
        mix[:, n * SLOT : (n + 1) * SLOT] = jnp.transpose(hit).astype(BF16)
    for n in range(0, NODES, 8):
        hits = [ones_where(rank_a[i : i + 1] == place_a) for i in range(n, n + 8)]
        mix_a[:, n * SLOT : (n + 8) * SLOT] = jnp.transpose(jnp.concatenate(hits, axis=0)).astype(BF16)
    for l in range(0, LOCALS, 2):
        hits = [jnp.where(seat[i : i + 1] == place_x, gain_a[i : i + 1], 0.0) for i in (l, l + 1)]
        merge[:, l * BAND : (l + 2) * BAND] = jnp.transpose(jnp.concatenate(hits, axis=0)).astype(BF16)

    def gate_up(q, get):
        s = q % SLOTS
        gate_load(0, s).wait()
        up_load(0, s).wait()
        for m in range(0, ROWS, ROW_TILE):
            rows = get(m)
            acc_g[m : m + ROW_TILE] += dot(rows, wgu[s, 0])
            acc_u[m : m + ROW_TILE] += dot(rows, wgu[s, 1])

        @pl.when(q + SLOTS < CHUNKS)
        def _():
            gate_load(in_turn(q + SLOTS), s).start()
            up_load(in_turn(q + SLOTS), s).start()

    @pl.loop(0, DIRECT)
    def _(i):
        for j in range(1, NODES):
            rows_copy(out1, in1, d_s, d_r, i, j).wait_recv()
        gate_up(2 * i, lambda m: in1[i, m : m + ROW_TILE])

        @pl.when(i < ONCE)
        def _():
            for k in range(1, LOCALS):
                pass_copy(i, k).wait_recv()
            for h in range(2):
                work[:, h * WIDE : (h + 1) * WIDE] = dot(square[...], xi[i, h * ROWS : (h + 1) * ROWS]).astype(BF16)
            gate_up(2 * i + 1, lambda m: work[m : m + ROW_TILE])
            acc_s[...] += dot(gathered(i), ws[columns(i), :])

    by_chip = quotient(row, BAND)
    by_node = quotient(row - by_chip * BAND, PART)
    square[...] = ones_where(row - by_chip * BAND - by_node * PART + by_node * SLOT + by_chip * PART == column).astype(BF16)
    for m in range(0, ROWS, ROW_TILE):
        hidden[m : m + ROW_TILE] = silu_mul(acc_g[m : m + ROW_TILE], acc_u[m : m + ROW_TILE]).astype(BF16)
    for m in range(0, ROWS, ROW_TILE):
        hidden_a[m : m + ROW_TILE] = dot(square[m : m + ROW_TILE], hidden[...]).astype(BF16)

    def back_copy(a, k):
        there = mate(k)
        return remote(
            xo.at[a, block(there % 2 * 4 + there // 2, BAND)], xe.at[a, block(local, BAND)],
            xc_s.at[a, k], xc_r.at[a, k], (node, there),
        )

    def next_down(c):
        @pl.when(c + SLOTS < CHUNKS)
        def _():
            down_load(c + SLOTS, c % SLOTS).start()

    @pl.loop(0, ONCE)
    def _(a):
        for k in range(1, LOCALS):
            pass_copy(a, k).wait_send()
        s = a % SLOTS
        down_load(0, s).wait()
        for h in range(2):
            xo[a, h * ROWS : (h + 1) * ROWS] = dot(hidden_a[...], wds[s, :, h * WIDE : (h + 1) * WIDE]).astype(BF16)
        next_down(a)
        for k in range(1, LOCALS):
            back_copy(a, k).start()
        xe[a, block(local, BAND)] = xo[a, block(core * 4 + x, BAND)]

    def node_sums(a):
        for j in range(1, NODES):
            rows_copy(ao, ai, ad_s, ad_r, a, j).wait_send()
        for k in range(1, LOCALS):
            back_copy(a, k).wait_recv()
        ao[a] = dot(merge[...], xe[a]).astype(BF16)
        for j in range(1, NODES):
            rows_copy(ao, ae, ac_s, ac_r, a, j).start()
        ae[a, mine] = ao[a, mine]

    @pl.loop(0, DIRECT)
    def _(b):
        for j in range(1, NODES):
            rows_copy(out1, in1, d_s, d_r, b, j).wait_send()
        c = b + ONCE
        s = c % SLOTS
        down_load(0, s).wait()
        out1[b] = dot(hidden[...], wds[s]).astype(BF16)
        next_down(c)
        for j in range(1, NODES):
            rows_copy(out1, in2, c_s, c_r, b, j).start()
        in2[b, mine] = out1[b, mine]

        @pl.when(b >= 1)
        def _():
            node_sums(b - 1)

    hid_s[...] = silu_mul(acc_s[:, :SHARE], acc_s[:, SHARE:]).astype(BF16)
    loads[2].wait()

    def sib_copy(c):
        return remote(held.at[c, 1 - core], from_sib.at[c], rs_s.at[c], rs_r.at[c], sib)

    def reduce_copy(c, k):
        return remote(
            held.at[c, core, tok_rows((x + k) % 4)], from_x.at[c, k], rx_s.at[c, k], rx_r.at[c, k], side(k)
        )

    def shared_part(c):
        for k in (1, 3, 2):
            gather_copy(c, k).wait_send()
        for k in range(4):
            forward_copy(c, k).wait_send()
        return dot(hid_s[...], wsd[:, columns(c)])

    def reduce(c):
        sib_copy(c).start()
        sib_copy(c).wait_recv()
        held[c, core] = (held[c, core].astype(F32) + from_sib[c].astype(F32)).astype(BF16)
        for k in (1, 3, 2):
            reduce_copy(c, k).start()

    def finish(c):
        total = held[c, core, tok_rows(x)].astype(F32)
        for k in (1, 3, 2):
            reduce_copy(c, k).wait_recv()
            total = total + from_x[c, k].astype(F32)
        out[:, columns(c)] = total.astype(BF16)

    @pl.loop(0, DIRECT)
    def _(i):
        for j in range(1, NODES):
            rows_copy(out1, in2, c_s, c_r, i, j).wait_recv()
        c = i + ONCE
        part = dot(mix[...], in2[i]) + shared_part(c)
        held[c] = part.astype(BF16).reshape(2, HALF, COLS)
        reduce(c)

        @pl.when(i >= 2)
        def _():
            finish(i - 2)

        @pl.when(i >= 1)
        def _():
            a = i - 1
            for j in range(1, NODES):
                rows_copy(ao, ae, ac_s, ac_r, a, j).wait_recv()
            held[a] = shared_part(a).astype(BF16).reshape(2, HALF, COLS)
            sums = dot(mix_a[...], ae[a])
            for h in range(2):
                old = held[a, h, tok_rows(x), wide].astype(F32)
                held[a, h, tok_rows(x), wide] = (old + sums[h * TOK : (h + 1) * TOK]).astype(BF16)
            reduce(a)

        finish(c)

    finish(ONCE - 1)

    @pl.loop(0, DIRECT)
    def _(b):
        for j in range(1, NODES):
            rows_copy(out1, in2, c_s, c_r, b, j).wait_send()

    @pl.loop(0, ONCE)
    def _(a):
        for k in range(1, LOCALS):
            back_copy(a, k).wait_send()
        for j in range(1, NODES):
            rows_copy(ao, ae, ac_s, ac_r, a, j).wait_send()

    @pl.loop(0, CHUNKS)
    def _(c):
        sib_copy(c).wait_send()
        for k in (1, 3, 2):
            reduce_copy(c, k).wait_send()


def on_device(tokens, ids, weights, *matrices):
    vmem = pl.BlockSpec(memory_space=pltpu.VMEM)
    hbm = pl.BlockSpec(memory_space=pl.ANY)
    dma = pltpu.SemaphoreType.DMA
    return pl.pallas_call(
        kernel,
        out_shape=jax.ShapeDtypeStruct((TOK, D), BF16),
        in_specs=[hbm, vmem, vmem] + [hbm] * 6,
        out_specs=vmem,
        scratch_shapes=[
            pltpu.VMEM((CHUNKS, 2, HALF, COLS), BF16),
            pltpu.VMEM((DIRECT, ROWS, COLS), BF16),
            pltpu.VMEM((DIRECT, ROWS, COLS), BF16),
            pltpu.VMEM((DIRECT, ROWS, COLS), BF16),
            pltpu.VMEM((ONCE, ROWS, WIDE), BF16),
            pltpu.VMEM((ONCE, ROWS, WIDE), BF16),
            pltpu.VMEM((ONCE, ROWS, WIDE), BF16),
            pltpu.VMEM((ONCE, SPREAD, WIDE), BF16),
            pltpu.VMEM((ONCE, SPREAD, WIDE), BF16),
            pltpu.VMEM((ONCE, SPREAD, WIDE), BF16),
            pltpu.VMEM((ROWS, H), F32),
            pltpu.VMEM((ROWS, H), F32),
            pltpu.VMEM((ROWS, H), BF16),
            pltpu.VMEM((ROWS, H), BF16),
            pltpu.VMEM((SLOTS, 2, COLS, H), BF16),
            pltpu.VMEM((SLOTS, H, COLS), BF16),
            pltpu.VMEM((D, 2 * SHARE), BF16),
            pltpu.VMEM((SHARE, D), BF16),
            pltpu.VMEM((GROUP, 2 * SHARE), F32),
            pltpu.VMEM((GROUP, SHARE), BF16),
            pltpu.VMEM((ROWS, GROUP), BF16),
            pltpu.VMEM((GROUP, ROWS), BF16),
            pltpu.VMEM((ROWS, PAIR), BF16),
            pltpu.VMEM((PAIR, ROWS), BF16),
            pltpu.VMEM((SPREAD, ROWS), BF16),
            pltpu.VMEM((ROWS, SPREAD), BF16),
            pltpu.VMEM((ROWS, ROWS), BF16),
            pltpu.VMEM((ROWS, COLS), BF16),
            pltpu.VMEM((2 * TOP, 128), F32),
            pltpu.VMEM((LOCALS, 2 * TOP, 128), F32),
            pltpu.VMEM((NODES, 2 * TOP, 128), F32),
            pltpu.VMEM((NODES, 2 * TOP, 128), F32),
            pltpu.VMEM((CHUNKS, HALF, COLS), BF16),
            pltpu.VMEM((CHUNKS, 4, TOK, COLS), BF16),
            dma((3,)),
            dma((SLOTS, 2)),
            dma((SLOTS,)),
            dma((CHUNKS,)),
            dma((LOCALS,)),
            dma((LOCALS,)),
            dma((NODES,)),
            dma((NODES,)),
            dma((CHUNKS, 4)),
            dma((CHUNKS, 4)),
            dma((CHUNKS, 4)),
            dma((CHUNKS, 4)),
            dma((DIRECT, NODES)),
            dma((DIRECT, NODES)),
            dma((DIRECT, NODES)),
            dma((DIRECT, NODES)),
            dma((ONCE, NODES)),
            dma((ONCE, NODES)),
            dma((ONCE, NODES)),
            dma((ONCE, NODES)),
            dma((ONCE, LOCALS)),
            dma((ONCE, LOCALS)),
            dma((ONCE, LOCALS)),
            dma((ONCE, LOCALS)),
            dma((CHUNKS,)),
            dma((CHUNKS,)),
            dma((CHUNKS, 4)),
            dma((CHUNKS, 4)),
        ],
        compiler_params=pltpu.CompilerParams(
            collective_id=0, has_side_effects=True, vmem_limit_bytes=63 * 2**20
        ),
        cost_estimate=pl.CostEstimate(flops=32 * 10**9, bytes_accessed=26 * 10**6, transcendentals=10**6),
        name="moe",
    )(tokens, ids.T, weights.T, *matrices)


def solution(mesh):
    both = ("node", "local")
    in_specs = (
        P(both, None),
        P(both, None),
        P(both, None),
        P(both, None, None),
        P(both, None, None),
        P(both, None, None),
        P(None, "local"),
        P(None, "local"),
        P("local", None),
    )
    return jax.shard_map(on_device, mesh=mesh, in_specs=in_specs, out_specs=P(both, None), check_vma=False)
```

```python
import jax
import jax.numpy as jnp
from jax import lax
from jax.experimental import pallas as pl
from jax.experimental.pallas import tpu as pltpu
from jax.sharding import PartitionSpec as P

MESH = pl.DeviceIdType.MESH
BF16 = jnp.bfloat16
F32 = jnp.float32

D = 3584
H = 1024
TOP = 8
TOK = 64
NODES = 16
LOCALS = 8
GROUP = TOK * LOCALS
PAIR = 2 * TOK
SLOT = 48
PART = 12
BAND = NODES * PART
ROWS = NODES * SLOT
SPREAD = LOCALS * BAND
COLS = 512
WIDE = COLS // 2
CHUNKS = D // COLS
ONCE = 3
DIRECT = CHUNKS - ONCE
HALF = GROUP // 2
SHARE = 128
ROW_TILE = 256
SLOTS = 3


def dot(a, b):
    return jnp.dot(a, b, preferred_element_type=F32)


def silu_mul(gate, up):
    return gate / (1.0 + jnp.exp(-gate)) * up


def count(shape, dim):
    return lax.broadcasted_iota(jnp.int32, shape, dim).astype(F32)


def quotient(values, by):
    return jnp.floor((values + 0.5) * (1.0 / by))


def ones_where(condition):
    return jnp.where(condition, 1.0, 0.0)


def kernel(
    tokens, ids, weights, eg, eu, ed, sg, su, sd, out,
    held, out1, in1, in2, ao, ai, ae, xo, xi, xe, acc_g, acc_u, hidden, hidden_a, wgu, wds, ws, wsd, acc_s, hid_s,
    pick, mix, pick_a, mix_a, spread, merge, square, work, meta, meta_all, slots_out, slots_in, from_sib, from_x, extra_out, extra,
    load_sem, gu_sem, wd_sem, own_sem, meta_s, meta_r, sm_s, sm_r, ag_s, ag_r, fw_s, fw_r,
    d_s, d_r, c_s, c_r, ad_s, ad_r, ac_s, ac_r, xd_s, xd_r, xc_s, xc_r, rs_s, rs_r, rx_s, rx_r, ex_s, ex_r,
):
    node = lax.axis_index("node")
    local = lax.axis_index("local")
    z, y, x, core = node // 4, node % 4, local // 2, local % 2
    sib = (node, 2 * x + (1 - core))

    def far(j):
        return ((z + j // 4) % 4) * 4 + (y + j % 4) % 4

    def side(k):
        return (node, 2 * ((x + k) % 4) + core)

    def mate(k):
        return (local + k) % LOCALS

    def block(i, size):
        return pl.ds(pl.multiple_of(i * size, size), size)

    def columns(c):
        return block(c, COLS)

    def tok_rows(i):
        return block(i, TOK)

    def remote(src, dst, send, recv, device):
        return pltpu.make_async_remote_copy(
            src_ref=src, dst_ref=dst, send_sem=send, recv_sem=recv, device_id=device, device_id_type=MESH
        )

    barrier = pltpu.get_barrier_semaphore()
    for j in range(1, NODES):
        pl.semaphore_signal(barrier, inc=1, device_id=(far(j), local), device_id_type=MESH)
    for k in range(1, LOCALS):
        pl.semaphore_signal(barrier, inc=1, device_id=(node, mate(k)), device_id_type=MESH)

    loads = [
        pltpu.make_async_copy(sg, ws.at[:, pl.ds(0, SHARE)], load_sem.at[0]),
        pltpu.make_async_copy(su, ws.at[:, pl.ds(SHARE, SHARE)], load_sem.at[1]),
        pltpu.make_async_copy(sd, wsd, load_sem.at[2]),
    ]

    def own_copy(c):
        return pltpu.make_async_copy(tokens.at[:, columns(c)], held.at[c, core, tok_rows(x)], own_sem.at[c])

    def gate_load(c, s):
        return pltpu.make_async_copy(eg.at[0, columns(c)], wgu.at[s, 0], gu_sem.at[s, 0])

    def up_load(c, s):
        return pltpu.make_async_copy(eu.at[0, columns(c)], wgu.at[s, 1], gu_sem.at[s, 1])

    def down_load(c, s):
        return pltpu.make_async_copy(ed.at[0, :, columns(c)], wds.at[s], wd_sem.at[s])

    def in_turn(q):
        return (q % 2 + q // (2 * ONCE)) * ONCE + q // 2

    for c in range(CHUNKS):
        own_copy(c).start()

    meta[...] = jnp.zeros_like(meta)
    meta[0:TOP, 0:TOK] = ids[...].astype(F32) + 1.0
    meta[TOP : 2 * TOP, 0:TOK] = weights[...].astype(F32)

    for load in loads:
        load.start()
    for s in range(SLOTS):
        gate_load(in_turn(s), s).start()
        up_load(in_turn(s), s).start()
    for s, c in enumerate((ONCE, 0, 1)):
        down_load(c, s).start()

    slots_out[...] = jnp.zeros_like(slots_out)
    acc_s[...] = jnp.zeros_like(acc_s)
    acc_g[...] = jnp.zeros_like(acc_g)
    acc_u[...] = jnp.zeros_like(acc_u)
    first, then = count((ROWS, 1), 0), count((1, ROWS), 1)
    earlier = (first < then) & (quotient(first, SLOT) == quotient(then, SLOT))
    square[...] = ones_where(earlier).astype(BF16)

    pl.semaphore_wait(barrier, NODES - 1 + LOCALS - 1)

    def meta_copy(k):
        return remote(meta, meta_all.at[core * 4 + x], meta_s.at[k], meta_r.at[k], (node, mate(k)))

    def gather_copy(c, k):
        return remote(tokens.at[:, columns(c)], held.at[c, core, tok_rows(x)], ag_s.at[c, k], ag_r.at[c, k], side(k))

    def forward_copy(c, k):
        mid = held.at[c, core, tok_rows((x + 4 - k) % 4)]
        return remote(tokens.at[:, columns(c)] if k == 0 else mid, mid, fw_s.at[c, k], fw_r.at[c, k], sib)

    for k in range(1, LOCALS):
        meta_copy(k).start()
    for c in range(CHUNKS):
        forward_copy(c, 0).start()

    @pl.loop(ONCE, CHUNKS)
    def _(c):
        for k in (1, 3, 2):
            gather_copy(c, k).start()

    meta_all[core * 4 + x] = meta[...]
    for k in range(1, LOCALS):
        meta_copy(k).wait()

    chip_table = jnp.concatenate([meta_all[x][:, :TOK], meta_all[4 + x][:, :TOK]], axis=1)
    chip_node = quotient(chip_table[:TOP] - 1.0, LOCALS)
    node_row = count((NODES, PAIR), 0)
    chosen = jnp.zeros((NODES, PAIR), F32)
    for k in range(0, TOP, 2):
        chosen = chosen + ones_where(chip_node[k : k + 1] == node_row)
    earlier = count((PAIR, PAIR), 0) < count((PAIR, PAIR), 1)
    rank_a = dot(chosen.astype(BF16), ones_where(earlier).astype(BF16))
    rank_a = jnp.where(chosen > 0.5, rank_a, -1.0)
    place_a = count((SLOT, PAIR), 0)
    for n in range(NODES):
        pick_a[n * SLOT : (n + 1) * SLOT] = ones_where(rank_a[n : n + 1] == place_a).astype(BF16)
    notes = lax.dot_general(
        chip_table.astype(BF16), pick_a[...], (((1,), (1,)), ((), ())), preferred_element_type=F32
    )
    for n in range(NODES):
        slots_out[n, :, 0:SLOT] = notes[:, n * SLOT : (n + 1) * SLOT]

    def notes_copy(j):
        there = far(j)
        return remote(slots_out.at[there], slots_in.at[node], sm_s.at[j], sm_r.at[j], (there, local))

    def rows_copy(src, dst, send, recv, c, j):
        there = far(j)
        return remote(
            src.at[c, block(there, SLOT)], dst.at[c, block(node, SLOT)], send.at[c, j], recv.at[c, j], (there, local)
        )

    mine = block(node, SLOT)
    wide = block(core, WIDE)

    for j in range(1, NODES):
        notes_copy(j).start()
    slots_in[node] = slots_out[node]

    @pl.loop(0, ONCE)
    def _(a):
        own_copy(a).wait()
        forward_copy(a, 0).wait_recv()
        rows = jnp.concatenate([held[a, 0, tok_rows(x), wide], held[a, 1, tok_rows(x), wide]], axis=0)
        ao[a] = dot(pick_a[...], rows).astype(BF16)
        for j in range(1, NODES):
            rows_copy(ao, ai, ad_s, ad_r, a, j).start()
        ai[a, mine] = ao[a, mine]

    table = jnp.concatenate([meta_all[d][:, :TOK] for d in range(LOCALS)], axis=1)
    expert = count((NODES, GROUP), 0) * LOCALS + (local + 1).astype(F32)
    chosen = jnp.zeros((NODES, GROUP), F32)
    gain = jnp.zeros((NODES, GROUP), F32)
    for k in range(TOP):
        hit = ones_where(table[k : k + 1] == expert)
        chosen = chosen + hit
        gain = gain + hit * table[TOP + k : TOP + k + 1]

    def chip_of(t):
        device = quotient(t, TOK)
        return device - 4.0 * quotient(device, 4)

    first, then = count((GROUP, 1), 0), count((1, GROUP), 1)
    earlier = (first < then) & (chip_of(first) == chip_of(then))
    rank = dot(chosen.astype(BF16), ones_where(earlier).astype(BF16)) + chip_of(then) * PART
    rank = jnp.where(chosen > 0.5, rank, -1.0)
    place = count((SLOT, GROUP), 0)
    for n in range(NODES):
        pick[n * SLOT : (n + 1) * SLOT] = ones_where(rank[n : n + 1] == place).astype(BF16)

    loads[0].wait()
    loads[1].wait()

    def hand_on(c):
        for k in (1, 3, 2):
            gather_copy(c, k).wait_recv()
            forward_copy(c, k).start()

    def gathered(c):
        for k in (1, 3, 2):
            forward_copy(c, k).wait_recv()
        return held[c].reshape(GROUP, COLS)

    def direct_rows(b):
        c = b + ONCE
        own_copy(c).wait()
        forward_copy(c, 0).wait_recv()
        hand_on(c)
        rows = gathered(c)
        out1[b] = dot(pick[...], rows).astype(BF16)
        for j in range(1, NODES):
            rows_copy(out1, in1, d_s, d_r, b, j).start()
        in1[b, mine] = out1[b, mine]
        acc_s[...] += dot(rows, ws[columns(c), :])

    def pass_copy(a, k):
        there = mate(k)
        return remote(
            xo.at[a, block(there, BAND)], xi.at[a, block(core * 4 + x, BAND)], xd_s.at[a, k], xd_r.at[a, k], (node, there)
        )

    def pass_rows(a):
        for j in range(1, NODES):
            rows_copy(ao, ai, ad_s, ad_r, a, j).wait_recv()
        xo[a] = dot(spread[...], ai[a]).astype(BF16)
        for k in range(1, LOCALS):
            pass_copy(a, k).start()
        xi[a, block(core * 4 + x, BAND)] = xo[a, block(local, BAND)]

    direct_rows(0)

    for j in range(1, NODES):
        notes_copy(j).wait()
    slot_table = jnp.concatenate([slots_in[n][:, :SLOT] for n in range(NODES)], axis=1)
    expert = count((LOCALS, ROWS), 0) + (node * LOCALS + 1).astype(F32)
    chosen = jnp.zeros((LOCALS, ROWS), F32)
    gain_a = jnp.zeros((LOCALS, ROWS), F32)
    for k in range(TOP):
        hit = ones_where(slot_table[k : k + 1] == expert)
        chosen = chosen + hit
        gain_a = gain_a + hit * slot_table[TOP + k : TOP + k + 1]
    slot_row = count((1, ROWS), 1)
    seat = dot(chosen.astype(BF16), square[...]) + quotient(slot_row, SLOT) * PART
    seat = jnp.where(chosen > 0.5, seat, -1.0)
    place_x = count((BAND, ROWS), 0)
    for l in range(LOCALS):
        spread[l * BAND : (l + 1) * BAND] = ones_where(seat[l : l + 1] == place_x).astype(BF16)

    @pl.loop(0, ONCE)
    def _(a):
        pass_rows(a)
        direct_rows(a + 1)

    @pl.loop(0, ONCE)
    def _(c):
        for k in (1, 3, 2):
            gather_copy(c, k).start()

    row, column = count((ROWS, 1), 0), count((1, ROWS), 1)
    by_node = quotient(row, SLOT)
    by_chip = quotient(row - by_node * SLOT, PART)
    square[...] = ones_where(row - by_node * SLOT - by_chip * PART + by_chip * BAND + by_node * PART == column).astype(BF16)
    for n in range(NODES):
        hit = jnp.where(rank[n : n + 1] == place, gain[n : n + 1], 0.0)
        mix[:, n * SLOT : (n + 1) * SLOT] = jnp.transpose(hit).astype(BF16)
    for n in range(0, NODES, 8):
        hits = [ones_where(rank_a[i : i + 1] == place_a) for i in range(n, n + 8)]
        mix_a[:, n * SLOT : (n + 8) * SLOT] = jnp.transpose(jnp.concatenate(hits, axis=0)).astype(BF16)
    for l in range(0, LOCALS, 2):
        hits = [jnp.where(seat[i : i + 1] == place_x, gain_a[i : i + 1], 0.0) for i in (l, l + 1)]
        merge[:, l * BAND : (l + 2) * BAND] = jnp.transpose(jnp.concatenate(hits, axis=0)).astype(BF16)

    def gate_up(q, get):
        s = q % SLOTS
        gate_load(0, s).wait()
        up_load(0, s).wait()
        for m in range(0, ROWS, ROW_TILE):
            rows = get(m)
            acc_g[m : m + ROW_TILE] += dot(rows, wgu[s, 0])
            acc_u[m : m + ROW_TILE] += dot(rows, wgu[s, 1])

        @pl.when(q + SLOTS < CHUNKS)
        def _():
            gate_load(in_turn(q + SLOTS), s).start()
            up_load(in_turn(q + SLOTS), s).start()

    @pl.loop(0, ONCE)
    def _(i):
        for k in range(1, LOCALS):
            pass_copy(i, k).wait_recv()
        for h in range(2):
            work[:, h * WIDE : (h + 1) * WIDE] = dot(square[...], xi[i, h * ROWS : (h + 1) * ROWS]).astype(BF16)
        gate_up(2 * i, lambda m: work[m : m + ROW_TILE])
        for j in range(1, NODES):
            rows_copy(out1, in1, d_s, d_r, i, j).wait_recv()
        gate_up(2 * i + 1, lambda m: in1[i, m : m + ROW_TILE])

    by_chip = quotient(row, BAND)
    by_node = quotient(row - by_chip * BAND, PART)
    square[...] = ones_where(row - by_chip * BAND - by_node * PART + by_node * SLOT + by_chip * PART == column).astype(BF16)

    for j in range(1, NODES):
        rows_copy(out1, in1, d_s, d_r, 0, j).wait_send()
    down_load(0, 0).wait()
    last = DIRECT - 1
    s_last = (CHUNKS - 1) % SLOTS
    gate_load(0, s_last).wait()
    up_load(0, s_last).wait()
    for j in range(1, NODES):
        rows_copy(out1, in1, d_s, d_r, last, j).wait_recv()

    @pl.loop(0, 4)
    def _(t):
        tile = block(t, BAND)
        rows = in1[last, tile]
        gate = acc_g[tile] + dot(rows, wgu[s_last, 0])
        up = acc_u[tile] + dot(rows, wgu[s_last, 1])
        hidden[tile] = silu_mul(gate, up).astype(BF16)
        out1[0, tile] = dot(hidden[tile], wds[0]).astype(BF16)
        for n in range(4):
            j = (t + 4 - z) % 4 * 4 + (n + 4 - y) % 4

            @pl.when(j != 0)
            def _():
                rows_copy(out1, in2, c_s, c_r, 0, j).start()

    in2[0, mine] = out1[0, mine]
    down_load(2, 0).start()
    for m in range(0, ROWS, ROW_TILE):
        hidden_a[m : m + ROW_TILE] = dot(square[m : m + ROW_TILE], hidden[...]).astype(BF16)

    def back_copy(a, k):
        there = mate(k)
        return remote(
            xo.at[a, block(there % 2 * 4 + there // 2, BAND)], xe.at[a, block(local, BAND)],
            xc_s.at[a, k], xc_r.at[a, k], (node, there),
        )

    @pl.loop(0, ONCE)
    def _(a):
        for k in range(1, LOCALS):
            pass_copy(a, k).wait_send()
        s = (a + 1) % SLOTS
        down_load(0, s).wait()
        for h in range(2):
            xo[a, h * ROWS : (h + 1) * ROWS] = dot(hidden_a[...], wds[s, :, h * WIDE : (h + 1) * WIDE]).astype(BF16)
        down_load(a + 4, s).start()
        for k in range(1, LOCALS):
            back_copy(a, k).start()
        xe[a, block(local, BAND)] = xo[a, block(core * 4 + x, BAND)]

    def node_sums(a):
        for j in range(1, NODES):
            rows_copy(ao, ai, ad_s, ad_r, a, j).wait_send()
        for k in range(1, LOCALS):
            back_copy(a, k).wait_recv()
        ao[a] = dot(merge[...], xe[a]).astype(BF16)
        for j in range(1, NODES):
            rows_copy(ao, ae, ac_s, ac_r, a, j).start()
        ae[a, mine] = ao[a, mine]

    def direct_back(b):
        for j in range(1, NODES):
            rows_copy(out1, in1, d_s, d_r, b, j).wait_send()
        s = b % SLOTS
        down_load(0, s).wait()
        out1[b] = dot(hidden[...], wds[s]).astype(BF16)
        for j in range(1, NODES):
            rows_copy(out1, in2, c_s, c_r, b, j).start()
        in2[b, mine] = out1[b, mine]

    direct_back(1)

    @pl.loop(0, ONCE)
    def _(a):
        hand_on(a)

    @pl.loop(0, 2)
    def _(a):
        node_sums(a)
        direct_back(a + 2)

    @pl.loop(0, ONCE)
    def _(a):
        acc_s[...] += dot(gathered(a), ws[columns(a), :])

    hid_s[...] = silu_mul(acc_s[:, :SHARE], acc_s[:, SHARE:]).astype(BF16)
    loads[2].wait()

    def sib_copy(c):
        return remote(held.at[c, 1 - core], from_sib.at[c], rs_s.at[c], rs_r.at[c], sib)

    def reduce_copy(c, k):
        return remote(
            held.at[c, core, tok_rows((x + k) % 4)], from_x.at[c, k], rx_s.at[c, k], rx_r.at[c, k], side(k)
        )

    def extra_copy(a):
        return remote(extra_out.at[a], extra.at[a, core], ex_s.at[a], ex_r.at[a], sib)

    def shared_part(c):
        for k in (1, 3, 2):
            gather_copy(c, k).wait_send()
        for k in range(4):
            forward_copy(c, k).wait_send()
        return dot(hid_s[...], wsd[:, columns(c)])

    def reduce(c):
        sib_copy(c).start()
        sib_copy(c).wait_recv()
        held[c, core] = (held[c, core].astype(F32) + from_sib[c].astype(F32)).astype(BF16)
        for k in (1, 3, 2):
            reduce_copy(c, k).start()

    def reduced(c):
        total = held[c, core, tok_rows(x)].astype(F32)
        for k in (1, 3, 2):
            reduce_copy(c, k).wait_recv()
            total = total + from_x[c, k].astype(F32)
        return total

    def finish(c):
        out[:, columns(c)] = reduced(c).astype(BF16)

    def finish_once(a):
        total = reduced(a)
        for j in range(1, NODES):
            rows_copy(ao, ae, ac_s, ac_r, a, j).wait_recv()
        sums = dot(mix_a[...], ae[a])
        extra_out[a] = jnp.where(core == 0, sums[TOK:], sums[:TOK])
        extra_copy(a).start()
        extra[a, core] = jnp.where(core == 0, sums[:TOK], sums[TOK:])
        extra_copy(a).wait_recv()
        out[:, columns(a)] = (total + jnp.concatenate([extra[a, 0], extra[a, 1]], axis=1)).astype(BF16)

    def direct_sums(b):
        for j in range(1, NODES):
            rows_copy(out1, in2, c_s, c_r, b, j).wait_recv()
        c = b + ONCE
        part = dot(mix[...], in2[b]) + shared_part(c)
        held[c] = part.astype(BF16).reshape(2, HALF, COLS)
        reduce(c)

    @pl.loop(0, ONCE)
    def _(a):
        held[a] = shared_part(a).astype(BF16).reshape(2, HALF, COLS)
        reduce(a)

    @pl.loop(0, 2)
    def _(b):
        direct_sums(b)

    node_sums(2)
    finish(ONCE)

    @pl.loop(0, 2)
    def _(i):
        finish_once(i)
        direct_sums(i + 2)
        finish(ONCE + i + 1)

    finish_once(2)
    finish(CHUNKS - 1)

    @pl.loop(0, DIRECT)
    def _(b):
        for j in range(1, NODES):
            rows_copy(out1, in2, c_s, c_r, b, j).wait_send()

    @pl.loop(0, ONCE)
    def _(a):
        for k in range(1, LOCALS):
            back_copy(a, k).wait_send()
        for j in range(1, NODES):
            rows_copy(ao, ae, ac_s, ac_r, a, j).wait_send()
        extra_copy(a).wait_send()

    @pl.loop(0, CHUNKS)
    def _(c):
        sib_copy(c).wait_send()
        for k in (1, 3, 2):
            reduce_copy(c, k).wait_send()


def on_device(tokens, ids, weights, *matrices):
    vmem = pl.BlockSpec(memory_space=pltpu.VMEM)
    hbm = pl.BlockSpec(memory_space=pl.ANY)
    dma = pltpu.SemaphoreType.DMA
    return pl.pallas_call(
        kernel,
        out_shape=jax.ShapeDtypeStruct((TOK, D), BF16),
        in_specs=[hbm, vmem, vmem] + [hbm] * 6,
        out_specs=vmem,
        scratch_shapes=[
            pltpu.VMEM((CHUNKS, 2, HALF, COLS), BF16),
            pltpu.VMEM((DIRECT, ROWS, COLS), BF16),
            pltpu.VMEM((DIRECT, ROWS, COLS), BF16),
            pltpu.VMEM((DIRECT, ROWS, COLS), BF16),
            pltpu.VMEM((ONCE, ROWS, WIDE), BF16),
            pltpu.VMEM((ONCE, ROWS, WIDE), BF16),
            pltpu.VMEM((ONCE, ROWS, WIDE), BF16),
            pltpu.VMEM((ONCE, SPREAD, WIDE), BF16),
            pltpu.VMEM((ONCE, SPREAD, WIDE), BF16),
            pltpu.VMEM((ONCE, SPREAD, WIDE), BF16),
            pltpu.VMEM((ROWS, H), F32),
            pltpu.VMEM((ROWS, H), F32),
            pltpu.VMEM((ROWS, H), BF16),
            pltpu.VMEM((ROWS, H), BF16),
            pltpu.VMEM((SLOTS, 2, COLS, H), BF16),
            pltpu.VMEM((SLOTS, H, COLS), BF16),
            pltpu.VMEM((D, 2 * SHARE), BF16),
            pltpu.VMEM((SHARE, D), BF16),
            pltpu.VMEM((GROUP, 2 * SHARE), F32),
            pltpu.VMEM((GROUP, SHARE), BF16),
            pltpu.VMEM((ROWS, GROUP), BF16),
            pltpu.VMEM((GROUP, ROWS), BF16),
            pltpu.VMEM((ROWS, PAIR), BF16),
            pltpu.VMEM((PAIR, ROWS), BF16),
            pltpu.VMEM((SPREAD, ROWS), BF16),
            pltpu.VMEM((ROWS, SPREAD), BF16),
            pltpu.VMEM((ROWS, ROWS), BF16),
            pltpu.VMEM((ROWS, COLS), BF16),
            pltpu.VMEM((2 * TOP, 128), F32),
            pltpu.VMEM((LOCALS, 2 * TOP, 128), F32),
            pltpu.VMEM((NODES, 2 * TOP, 128), F32),
            pltpu.VMEM((NODES, 2 * TOP, 128), F32),
            pltpu.VMEM((CHUNKS, HALF, COLS), BF16),
            pltpu.VMEM((CHUNKS, 4, TOK, COLS), BF16),
            pltpu.VMEM((ONCE, TOK, WIDE), F32),
            pltpu.VMEM((ONCE, 2, TOK, WIDE), F32),
            dma((3,)),
            dma((SLOTS, 2)),
            dma((SLOTS,)),
            dma((CHUNKS,)),
            dma((LOCALS,)),
            dma((LOCALS,)),
            dma((NODES,)),
            dma((NODES,)),
            dma((CHUNKS, 4)),
            dma((CHUNKS, 4)),
            dma((CHUNKS, 4)),
            dma((CHUNKS, 4)),
            dma((DIRECT, NODES)),
            dma((DIRECT, NODES)),
            dma((DIRECT, NODES)),
            dma((DIRECT, NODES)),
            dma((ONCE, NODES)),
            dma((ONCE, NODES)),
            dma((ONCE, NODES)),
            dma((ONCE, NODES)),
            dma((ONCE, LOCALS)),
            dma((ONCE, LOCALS)),
            dma((ONCE, LOCALS)),
            dma((ONCE, LOCALS)),
            dma((CHUNKS,)),
            dma((CHUNKS,)),
            dma((CHUNKS, 4)),
            dma((CHUNKS, 4)),
            dma((ONCE,)),
            dma((ONCE,)),
        ],
        compiler_params=pltpu.CompilerParams(
            collective_id=0, has_side_effects=True, vmem_limit_bytes=63 * 2**20
        ),
        cost_estimate=pl.CostEstimate(flops=32 * 10**9, bytes_accessed=26 * 10**6, transcendentals=10**6),
        name="moe",
    )(tokens, ids.T, weights.T, *matrices)


def solution(mesh):
    both = ("node", "local")
    in_specs = (
        P(both, None),
        P(both, None),
        P(both, None),
        P(both, None, None),
        P(both, None, None),
        P(both, None, None),
        P(None, "local"),
        P(None, "local"),
        P("local", None),
    )
    return jax.shard_map(on_device, mesh=mesh, in_specs=in_specs, out_specs=P(both, None), check_vma=False)
```

```python
import jax
import jax.numpy as jnp
from jax import lax
from jax.experimental import pallas as pl
from jax.experimental.pallas import tpu as pltpu
from jax.sharding import PartitionSpec as P

MESH = pl.DeviceIdType.MESH
BF16 = jnp.bfloat16
F32 = jnp.float32

D = 3584
H = 1024
TOP = 8
TOK = 64
NODES = 16
LOCALS = 8
GROUP = TOK * LOCALS
PAIR = 2 * TOK
SLOT = 48
PART = 12
BAND = NODES * PART
ROWS = NODES * SLOT
SPREAD = LOCALS * BAND
COLS = 512
WIDE = COLS // 2
CHUNKS = D // COLS
ONCE = 3
DIRECT = CHUNKS - ONCE
HALF = GROUP // 2
SHARE = 128
ROW_TILE = 256
SLOTS = 3


def dot(a, b):
    return jnp.dot(a, b, preferred_element_type=F32)


def silu_mul(gate, up):
    return gate / (1.0 + jnp.exp(-gate)) * up


def count(shape, dim):
    return lax.broadcasted_iota(jnp.int32, shape, dim).astype(F32)


def quotient(values, by):
    return jnp.floor((values + 0.5) * (1.0 / by))


def ones_where(condition):
    return jnp.where(condition, 1.0, 0.0)


def kernel(
    tokens, ids, weights, eg, eu, ed, sg, su, sd, out,
    held, out1, in1, in2, ao, ai, ae, xo, xi, xe, acc_g, acc_u, hidden, hidden_a, wgu, wds, ws, wsd, acc_s, hid_s,
    pick, mix, pick_a, mix_a, spread, merge, square, work, meta, meta_all, slots_out, slots_in, from_sib, from_x, extra_out, extra, out_v,
    load_sem, gu_sem, wd_sem, own_sem, meta_s, meta_r, sm_s, sm_r, ag_s, ag_r, fw_s, fw_r, own_s, own_r,
    d_s, d_r, c_s, c_r, ad_s, ad_r, ac_s, ac_r, xd_s, xd_r, xc_s, xc_r, rs_s, rs_r, rx_s, rx_r, ex_s, ex_r, out_sem,
):
    node = lax.axis_index("node")
    local = lax.axis_index("local")
    z, y, x, core = node // 4, node % 4, local // 2, local % 2
    sib = (node, 2 * x + (1 - core))

    def far(j):
        return ((z + j // 4) % 4) * 4 + (y + j % 4) % 4

    def side(k):
        return (node, 2 * ((x + k) % 4) + core)

    def mate(k):
        return (local + k) % LOCALS

    def block(i, size):
        return pl.ds(pl.multiple_of(i * size, size), size)

    def by_tiles(rows, work_on):
        @pl.loop(0, rows // ROW_TILE)
        def _(i):
            work_on(block(i, ROW_TILE))

    def columns(c):
        return block(c, COLS)

    def tok_rows(i):
        return block(i, TOK)

    def remote(src, dst, send, recv, device):
        return pltpu.make_async_remote_copy(
            src_ref=src, dst_ref=dst, send_sem=send, recv_sem=recv, device_id=device, device_id_type=MESH
        )

    def settled(ref, sem):
        pltpu.make_async_copy(ref, ref, sem).wait()

    barrier = pltpu.get_barrier_semaphore()
    for j in range(1, NODES):
        pl.semaphore_signal(barrier, inc=1, device_id=(far(j), local), device_id_type=MESH)
    for k in range(1, LOCALS):
        pl.semaphore_signal(barrier, inc=1, device_id=(node, mate(k)), device_id_type=MESH)

    loads = [
        pltpu.make_async_copy(sg, ws.at[:, pl.ds(0, SHARE)], load_sem.at[0]),
        pltpu.make_async_copy(su, ws.at[:, pl.ds(SHARE, SHARE)], load_sem.at[1]),
        pltpu.make_async_copy(sd, wsd, load_sem.at[2]),
    ]

    def own_copy(c):
        return pltpu.make_async_copy(tokens.at[:, columns(c)], held.at[c, core, tok_rows(x)], own_sem.at[c])

    def gate_load(c, s):
        return pltpu.make_async_copy(eg.at[0, columns(c)], wgu.at[s, 0], gu_sem.at[s, 0])

    def up_load(c, s):
        return pltpu.make_async_copy(eu.at[0, columns(c)], wgu.at[s, 1], gu_sem.at[s, 1])

    def down_load(c, s):
        return pltpu.make_async_copy(ed.at[0, :, columns(c)], wds.at[s], wd_sem.at[s])

    def in_turn(q):
        return (1 - q % 2) * ONCE + q // 2

    for c in range(CHUNKS):
        own_copy(c).start()

    meta[...] = jnp.zeros_like(meta)
    meta[0:TOP, 0:TOK] = ids[...].astype(F32) + 1.0
    meta[TOP : 2 * TOP, 0:TOK] = weights[...].astype(F32)

    pl.semaphore_wait(barrier, NODES - 1 + LOCALS - 1)

    def meta_copy(k, s):
        return remote(meta, meta_all.at[core * 4 + x], meta_s.at[s], meta_r.at[s], (node, mate(k)))

    def gather_copy(c, k):
        return remote(tokens.at[:, columns(c)], held.at[c, core, tok_rows(x)], ag_s.at[c], ag_r.at[c], side(k))

    def forward_copy(c, k):
        mid = held.at[c, core, tok_rows((x + 4 - k) % 4)]
        if k == 0:
            return remote(tokens.at[:, columns(c)], mid, own_s.at[c], own_r.at[c], sib)
        return remote(mid, mid, fw_s.at[c], fw_r.at[c], sib)

    def three_wait(sem, c):
        settled(held.at[c, 0, pl.ds(0, 3 * TOK)], sem.at[c])

    to_sib = 1 + 6 * core
    meta_copy(to_sib, 0).start()
    for c in range(CHUNKS):
        forward_copy(c, 0).start()
    for k in range(2, LOCALS - 1):
        meta_copy(k, 1).start()
    meta_copy(LOCALS - to_sib, 1).start()

    @pl.loop(0, CHUNKS)
    def _(i):
        for k in (1, 3, 2):
            gather_copy((i + ONCE) % CHUNKS, k).start()

    meta_all[core * 4 + x] = meta[...]
    meta_copy(to_sib, 0).wait_recv()

    chip_table = jnp.concatenate([meta_all[x][:, :TOK], meta_all[4 + x][:, :TOK]], axis=1)
    chip_node = quotient(chip_table[:TOP] - 1.0, LOCALS)
    node_row = count((NODES, PAIR), 0)
    chosen = jnp.zeros((NODES, PAIR), F32)
    for k in range(0, TOP, 2):
        chosen = chosen + ones_where(chip_node[k : k + 1] == node_row)
    earlier = count((PAIR, PAIR), 0) < count((PAIR, PAIR), 1)
    rank_a = dot(chosen.astype(BF16), ones_where(earlier).astype(BF16))
    rank_a = jnp.where(chosen > 0.5, rank_a, -1.0)
    place_a = count((SLOT, PAIR), 0)
    for n in range(NODES):
        pick_a[n * SLOT : (n + 1) * SLOT] = ones_where(rank_a[n : n + 1] == place_a).astype(BF16)

    def notes_copy(j):
        there = far(j)
        return remote(slots_out.at[there], slots_in.at[node], sm_s.at[0], sm_r.at[0], (there, local))

    def rows_copy(src, dst, send, recv, c, j):
        there = far(j)
        return remote(
            src.at[c, block(there, SLOT)], dst.at[c, block(node, SLOT)], send.at[c], recv.at[c], (there, local)
        )

    def rows_wait(ref, sem, c):
        settled(ref.at[c, pl.ds(0, (NODES - 1) * SLOT)], sem.at[c])

    def lanes_wait(ref, sem, a):
        settled(ref.at[a, pl.ds(0, (LOCALS - 1) * BAND)], sem.at[a])

    mine = block(node, SLOT)
    wide = block(core, WIDE)

    def once_rows(a):
        own_copy(a).wait()
        forward_copy(a, 0).wait_recv()
        rows = jnp.concatenate([held[a, 0, tok_rows(x), wide], held[a, 1, tok_rows(x), wide]], axis=0)
        ao[a] = dot(pick_a[...], rows).astype(BF16)
        for j in range(1, NODES):
            rows_copy(ao, ai, ad_s, ad_r, a, j).start()
        ai[a, mine] = ao[a, mine]

    once_rows(0)

    slots_out[...] = jnp.zeros_like(slots_out)
    notes = lax.dot_general(
        chip_table.astype(BF16), pick_a[...], (((1,), (1,)), ((), ())), preferred_element_type=F32
    )
    for n in range(NODES):
        slots_out[n, :, 0:SLOT] = notes[:, n * SLOT : (n + 1) * SLOT]

    for j in range(1, NODES):
        notes_copy(j).start()
    slots_in[node] = slots_out[node]

    @pl.loop(1, ONCE)
    def _(a):
        once_rows(a)

    for load in loads:
        load.start()
    for s in range(SLOTS):
        gate_load(in_turn(s), s).start()
        up_load(in_turn(s), s).start()
    for s, c in enumerate((ONCE, 0, 1)):
        down_load(c, s).start()

    def hand_on(c):
        three_wait(ag_r, c)
        for k in (1, 3, 2):
            forward_copy(c, k).start()

    def gathered(c):
        three_wait(fw_r, c)

    def shared_add(c):
        @pl.loop(0, 2)
        def _(h):
            acc_s[block(h, HALF)] += dot(held[c, h], ws[columns(c), :])

    def direct_rows(b):
        c = b + ONCE
        own_copy(c).wait()
        forward_copy(c, 0).wait_recv()
        hand_on(c)
        gathered(c)

        def select(tile):
            out1[b, tile] = dot(pick[tile], held[c].reshape(GROUP, COLS)).astype(BF16)

        by_tiles(ROWS, select)
        for j in range(1, NODES):
            rows_copy(out1, in1, d_s, d_r, b, j).start()
        in1[b, mine] = out1[b, mine]
        shared_add(c)

    def pass_copy(a, k):
        there = mate(k)
        return remote(
            xo.at[a, block(there, BAND)], xi.at[a, block(core * 4 + x, BAND)], xd_s.at[a], xd_r.at[a], (node, there)
        )

    def pass_rows(a):
        rows_wait(ai, ad_r, a)

        def select(tile):
            xo[a, tile] = dot(spread[tile], ai[a]).astype(BF16)

        by_tiles(SPREAD, select)
        for k in range(1, LOCALS):
            pass_copy(a, k).start()
        xi[a, block(core * 4 + x, BAND)] = xo[a, block(local, BAND)]

    first, then = count((ROWS, 1), 0), count((1, ROWS), 1)
    earlier = (first < then) & (quotient(first, SLOT) == quotient(then, SLOT))
    square[...] = ones_where(earlier).astype(BF16)

    settled(slots_in.at[pl.ds(0, NODES - 1)], sm_s.at[0])
    settled(slots_in.at[pl.ds(0, NODES - 1)], sm_r.at[0])
    slot_table = jnp.concatenate([slots_in[n][:, :SLOT] for n in range(NODES)], axis=1)
    expert = count((LOCALS, ROWS), 0) + (node * LOCALS + 1).astype(F32)
    chosen = jnp.zeros((LOCALS, ROWS), F32)
    gain_a = jnp.zeros((LOCALS, ROWS), F32)
    for k in range(TOP):
        hit = ones_where(slot_table[k : k + 1] == expert)
        chosen = chosen + hit
        gain_a = gain_a + hit * slot_table[TOP + k : TOP + k + 1]
    slot_row = count((1, ROWS), 1)
    seat = dot(chosen.astype(BF16), square[...]) + quotient(slot_row, SLOT) * PART
    seat = jnp.where(chosen > 0.5, seat, -1.0)
    place_x = count((BAND, ROWS), 0)
    for l in range(LOCALS):
        spread[l * BAND : (l + 1) * BAND] = ones_where(seat[l : l + 1] == place_x).astype(BF16)

    meta_copy(to_sib, 0).wait_send()
    settled(meta_all.at[pl.ds(0, LOCALS - 2)], meta_s.at[1])
    settled(meta_all.at[pl.ds(0, LOCALS - 2)], meta_r.at[1])

    table = jnp.concatenate([meta_all[d][:, :TOK] for d in range(LOCALS)], axis=1)
    expert = count((NODES, GROUP), 0) * LOCALS + (local + 1).astype(F32)
    chosen = jnp.zeros((NODES, GROUP), F32)
    gain = jnp.zeros((NODES, GROUP), F32)
    for k in range(TOP):
        hit = ones_where(table[k : k + 1] == expert)
        chosen = chosen + hit
        gain = gain + hit * table[TOP + k : TOP + k + 1]

    def chip_of(t):
        device = quotient(t, TOK)
        return device - 4.0 * quotient(device, 4)

    first, then = count((GROUP, 1), 0), count((1, GROUP), 1)
    earlier = (first < then) & (chip_of(first) == chip_of(then))
    rank = dot(chosen.astype(BF16), ones_where(earlier).astype(BF16)) + chip_of(then) * PART
    rank = jnp.where(chosen > 0.5, rank, -1.0)
    place = count((SLOT, GROUP), 0)
    for n in range(NODES):
        pick[n * SLOT : (n + 1) * SLOT] = ones_where(rank[n : n + 1] == place).astype(BF16)

    acc_s[...] = jnp.zeros_like(acc_s)
    loads[0].wait()
    loads[1].wait()

    @pl.loop(0, DIRECT)
    def _(b):
        @pl.when(b < ONCE)
        def _():
            pass_rows(b)

        direct_rows(b)

    @pl.loop(0, ONCE)
    def _(a):
        hand_on(a)

    @pl.loop(0, ONCE)
    def _(a):
        gathered(a)
        shared_add(a)

    hid_s[...] = silu_mul(acc_s[:, :SHARE], acc_s[:, SHARE:]).astype(BF16)
    loads[2].wait()

    def sib_copy(c):
        return remote(held.at[c, 1 - core], from_sib.at[c], rs_s.at[c], rs_r.at[c], sib)

    def reduce_copy(c, k):
        return remote(
            held.at[c, core, tok_rows((x + k) % 4)], from_x.at[c, k], rx_s.at[c], rx_r.at[c], side(k)
        )

    def extra_copy(a):
        return remote(extra_out.at[a], extra.at[a, core], ex_s.at[a], ex_r.at[a], sib)

    def gather_sent(c):
        three_wait(ag_s, c)
        three_wait(fw_s, c)
        forward_copy(c, 0).wait_send()

    def shared_part(c, h):
        return dot(hid_s[block(h, HALF)], wsd[:, columns(c)])

    def reduce(c):
        sib_copy(c).start()
        sib_copy(c).wait_recv()
        held[c, core] = (held[c, core].astype(F32) + from_sib[c].astype(F32)).astype(BF16)
        for k in (1, 3, 2):
            reduce_copy(c, k).start()

    def reduced(c):
        total = held[c, core, tok_rows(x)].astype(F32)
        settled(from_x.at[c, pl.ds(1, 3)], rx_r.at[c])
        for k in (1, 3, 2):
            total = total + from_x[c, k].astype(F32)
        return total

    def out_copy(c):
        return pltpu.make_async_copy(out_v.at[c], out.at[:, columns(c)], out_sem.at[c])

    def finish(c):
        out_v[c] = reduced(c).astype(BF16)
        out_copy(c).start()

    def finish_once(a):
        total = reduced(a)
        rows_wait(ae, ac_r, a)
        sums = dot(mix_a[...], ae[a])
        extra_out[a] = jnp.where(core == 0, sums[TOK:], sums[:TOK])
        extra_copy(a).start()
        extra[a, core] = jnp.where(core == 0, sums[:TOK], sums[TOK:])
        extra_copy(a).wait_recv()
        out_v[a] = (total + jnp.concatenate([extra[a, 0], extra[a, 1]], axis=1)).astype(BF16)
        out_copy(a).start()

    def direct_sums(b):
        rows_wait(in2, c_r, b)
        c = b + ONCE
        gather_sent(c)

        @pl.loop(0, 2)
        def _(h):
            held[c, h] = (dot(mix[block(h, HALF)], in2[b]) + shared_part(c, h)).astype(BF16)

        reduce(c)

    @pl.loop(0, ONCE)
    def _(a):
        gather_sent(a)

        @pl.loop(0, 2)
        def _(h):
            held[a, h] = shared_part(a, h).astype(BF16)

        reduce(a)

    def clear(tile):
        acc_g[tile] = jnp.zeros((ROW_TILE, H), F32)
        acc_u[tile] = jnp.zeros((ROW_TILE, H), F32)

    by_tiles(ROWS, clear)

    row, column = count((ROWS, 1), 0), count((1, ROWS), 1)
    by_node = quotient(row, SLOT)
    by_chip = quotient(row - by_node * SLOT, PART)
    square[...] = ones_where(row - by_node * SLOT - by_chip * PART + by_chip * BAND + by_node * PART == column).astype(BF16)
    for n in range(NODES):
        hit = jnp.where(rank[n : n + 1] == place, gain[n : n + 1], 0.0)
        mix[:, n * SLOT : (n + 1) * SLOT] = jnp.transpose(hit).astype(BF16)
    for n in range(0, NODES, 8):
        hits = [ones_where(rank_a[i : i + 1] == place_a) for i in range(n, n + 8)]
        mix_a[:, n * SLOT : (n + 8) * SLOT] = jnp.transpose(jnp.concatenate(hits, axis=0)).astype(BF16)
    for l in range(0, LOCALS, 2):
        hits = [jnp.where(seat[i : i + 1] == place_x, gain_a[i : i + 1], 0.0) for i in (l, l + 1)]
        merge[:, l * BAND : (l + 2) * BAND] = jnp.transpose(jnp.concatenate(hits, axis=0)).astype(BF16)

    def gate_up(q, get):
        s = q % SLOTS
        gate_load(0, s).wait()
        up_load(0, s).wait()

        def add(tile):
            rows = get(tile)
            acc_g[tile] += dot(rows, wgu[s, 0])
            acc_u[tile] += dot(rows, wgu[s, 1])

        by_tiles(ROWS, add)

        @pl.when(q + SLOTS < CHUNKS)
        def _():
            gate_load(in_turn(q + SLOTS), s).start()
            up_load(in_turn(q + SLOTS), s).start()

    @pl.loop(0, ONCE)
    def _(i):
        rows_wait(in1, d_r, i)
        gate_up(2 * i, lambda tile: in1[i, tile])
        lanes_wait(xi, xd_r, i)

        def reorder(tile):
            for h in range(2):
                work[tile, h * WIDE : (h + 1) * WIDE] = dot(square[tile], xi[i, h * ROWS : (h + 1) * ROWS]).astype(BF16)

        by_tiles(ROWS, reorder)
        gate_up(2 * i + 1, lambda tile: work[tile])

    by_chip = quotient(row, BAND)
    by_node = quotient(row - by_chip * BAND, PART)
    square[...] = ones_where(row - by_chip * BAND - by_node * PART + by_node * SLOT + by_chip * PART == column).astype(BF16)

    rows_wait(out1, d_s, 0)
    down_load(0, 0).wait()
    last = DIRECT - 1
    s_last = (CHUNKS - 1) % SLOTS
    gate_load(0, s_last).wait()
    up_load(0, s_last).wait()
    rows_wait(in1, d_r, last)

    @pl.loop(0, 4)
    def _(t):
        tile = block(t, BAND)
        rows = in1[last, tile]
        gate = acc_g[tile] + dot(rows, wgu[s_last, 0])
        up = acc_u[tile] + dot(rows, wgu[s_last, 1])
        hidden[tile] = silu_mul(gate, up).astype(BF16)
        out1[0, tile] = dot(hidden[tile], wds[0]).astype(BF16)
        for n in range(4):
            j = (t + 4 - z) % 4 * 4 + (n + 4 - y) % 4

            @pl.when(j != 0)
            def _():
                rows_copy(out1, in2, c_s, c_r, 0, j).start()

    in2[0, mine] = out1[0, mine]
    down_load(2, 0).start()

    def reorder_hidden(tile):
        hidden_a[tile] = dot(square[tile], hidden[...]).astype(BF16)

    by_tiles(ROWS, reorder_hidden)

    def back_copy(a, k):
        there = mate(k)
        return remote(
            xo.at[a, block(there % 2 * 4 + there // 2, BAND)], xe.at[a, block(local, BAND)],
            xc_s.at[a], xc_r.at[a], (node, there),
        )

    @pl.loop(0, ONCE)
    def _(a):
        lanes_wait(xo, xd_s, a)
        s = (a + 1) % SLOTS
        down_load(0, s).wait()

        @pl.loop(0, ROWS // ROW_TILE)
        def _(i):
            for h in range(2):
                part = dot(hidden_a[block(i, ROW_TILE)], wds[s, :, h * WIDE : (h + 1) * WIDE])
                xo[a, block(h * (ROWS // ROW_TILE) + i, ROW_TILE)] = part.astype(BF16)

        down_load(a + 4, s).start()
        for k in range(1, LOCALS):
            back_copy(a, k).start()
        xe[a, block(local, BAND)] = xo[a, block(core * 4 + x, BAND)]

    def node_sums(a):
        rows_wait(ao, ad_s, a)
        lanes_wait(xe, xc_r, a)

        def add(tile):
            ao[a, tile] = dot(merge[tile], xe[a]).astype(BF16)

        by_tiles(ROWS, add)
        for j in range(1, NODES):
            rows_copy(ao, ae, ac_s, ac_r, a, j).start()
        ae[a, mine] = ao[a, mine]

    def direct_back(b):
        rows_wait(out1, d_s, b)
        s = b % SLOTS
        down_load(0, s).wait()

        def down(tile):
            out1[b, tile] = dot(hidden[tile], wds[s]).astype(BF16)

        by_tiles(ROWS, down)
        for j in range(1, NODES):
            rows_copy(out1, in2, c_s, c_r, b, j).start()
        in2[b, mine] = out1[b, mine]

    @pl.loop(1, DIRECT)
    def _(b):
        @pl.when(b > 1)
        def _():
            node_sums(b - 2)

        direct_back(b)

    @pl.loop(0, DIRECT)
    def _(b):
        @pl.when(b == 2)
        def _():
            node_sums(ONCE - 1)

        @pl.when(b >= 2)
        def _():
            finish_once(b - 2)

        direct_sums(b)

        @pl.when(b >= 1)
        def _():
            finish(ONCE + b - 1)

    finish_once(ONCE - 1)
    finish(CHUNKS - 1)

    @pl.loop(0, DIRECT)
    def _(b):
        rows_wait(out1, c_s, b)

    @pl.loop(0, ONCE)
    def _(a):
        lanes_wait(xo, xc_s, a)
        rows_wait(ao, ac_s, a)
        extra_copy(a).wait_send()

    @pl.loop(0, CHUNKS)
    def _(c):
        sib_copy(c).wait_send()
        settled(from_x.at[c, pl.ds(1, 3)], rx_s.at[c])
        out_copy(c).wait()


def on_device(tokens, ids, weights, *matrices):
    vmem = pl.BlockSpec(memory_space=pltpu.VMEM)
    hbm = pl.BlockSpec(memory_space=pl.ANY)
    dma = pltpu.SemaphoreType.DMA
    return pl.pallas_call(
        kernel,
        out_shape=jax.ShapeDtypeStruct((TOK, D), BF16),
        in_specs=[hbm, vmem, vmem] + [hbm] * 6,
        out_specs=hbm,
        scratch_shapes=[
            pltpu.VMEM((CHUNKS, 2, HALF, COLS), BF16),
            pltpu.VMEM((DIRECT, ROWS, COLS), BF16),
            pltpu.VMEM((DIRECT, ROWS, COLS), BF16),
            pltpu.VMEM((DIRECT, ROWS, COLS), BF16),
            pltpu.VMEM((ONCE, ROWS, WIDE), BF16),
            pltpu.VMEM((ONCE, ROWS, WIDE), BF16),
            pltpu.VMEM((ONCE, ROWS, WIDE), BF16),
            pltpu.VMEM((ONCE, SPREAD, WIDE), BF16),
            pltpu.VMEM((ONCE, SPREAD, WIDE), BF16),
            pltpu.VMEM((ONCE, SPREAD, WIDE), BF16),
            pltpu.VMEM((ROWS, H), F32),
            pltpu.VMEM((ROWS, H), F32),
            pltpu.VMEM((ROWS, H), BF16),
            pltpu.VMEM((ROWS, H), BF16),
            pltpu.VMEM((SLOTS, 2, COLS, H), BF16),
            pltpu.VMEM((SLOTS, H, COLS), BF16),
            pltpu.VMEM((D, 2 * SHARE), BF16),
            pltpu.VMEM((SHARE, D), BF16),
            pltpu.VMEM((GROUP, 2 * SHARE), F32),
            pltpu.VMEM((GROUP, SHARE), BF16),
            pltpu.VMEM((ROWS, GROUP), BF16),
            pltpu.VMEM((GROUP, ROWS), BF16),
            pltpu.VMEM((ROWS, PAIR), BF16),
            pltpu.VMEM((PAIR, ROWS), BF16),
            pltpu.VMEM((SPREAD, ROWS), BF16),
            pltpu.VMEM((ROWS, SPREAD), BF16),
            pltpu.VMEM((ROWS, ROWS), BF16),
            pltpu.VMEM((ROWS, COLS), BF16),
            pltpu.VMEM((2 * TOP, 128), F32),
            pltpu.VMEM((LOCALS, 2 * TOP, 128), F32),
            pltpu.VMEM((NODES, 2 * TOP, 128), F32),
            pltpu.VMEM((NODES, 2 * TOP, 128), F32),
            pltpu.VMEM((CHUNKS, HALF, COLS), BF16),
            pltpu.VMEM((CHUNKS, 4, TOK, COLS), BF16),
            pltpu.VMEM((ONCE, TOK, WIDE), F32),
            pltpu.VMEM((ONCE, 2, TOK, WIDE), F32),
            pltpu.VMEM((CHUNKS, TOK, COLS), BF16),
            dma((3,)),
            dma((SLOTS, 2)),
            dma((SLOTS,)),
            dma((CHUNKS,)),
            dma((2,)),
            dma((2,)),
            dma((1,)),
            dma((1,)),
            dma((CHUNKS,)),
            dma((CHUNKS,)),
            dma((CHUNKS,)),
            dma((CHUNKS,)),
            dma((CHUNKS,)),
            dma((CHUNKS,)),
            dma((DIRECT,)),
            dma((DIRECT,)),
            dma((DIRECT,)),
            dma((DIRECT,)),
            dma((ONCE,)),
            dma((ONCE,)),
            dma((ONCE,)),
            dma((ONCE,)),
            dma((ONCE,)),
            dma((ONCE,)),
            dma((ONCE,)),
            dma((ONCE,)),
            dma((CHUNKS,)),
            dma((CHUNKS,)),
            dma((CHUNKS,)),
            dma((CHUNKS,)),
            dma((ONCE,)),
            dma((ONCE,)),
            dma((CHUNKS,)),
        ],
        compiler_params=pltpu.CompilerParams(
            collective_id=0, has_side_effects=True, vmem_limit_bytes=63 * 2**20
        ),
        cost_estimate=pl.CostEstimate(flops=32 * 10**9, bytes_accessed=26 * 10**6, transcendentals=10**6),
        name="moe",
    )(tokens, ids.T, weights.T, *matrices)


def solution(mesh):
    both = ("node", "local")
    in_specs = (
        P(both, None),
        P(both, None),
        P(both, None),
        P(both, None, None),
        P(both, None, None),
        P(both, None, None),
        P(None, "local"),
        P(None, "local"),
        P("local", None),
    )
    return jax.shard_map(on_device, mesh=mesh, in_specs=in_specs, out_specs=P(both, None), check_vma=False)
```

```python
import jax
import jax.numpy as jnp
from jax import lax
from jax.experimental import pallas as pl
from jax.experimental.pallas import tpu as pltpu
from jax.sharding import PartitionSpec as P

MESH = pl.DeviceIdType.MESH
BF16 = jnp.bfloat16
F32 = jnp.float32

D = 3584
H = 1024
TOP = 8
TOK = 64
NODES = 16
LOCALS = 8
GROUP = TOK * LOCALS
PAIR = 2 * TOK
SLOT = 48
PART = 12
BAND = NODES * PART
ROWS = NODES * SLOT
SPREAD = LOCALS * BAND
COLS = 512
WIDE = COLS // 2
CHUNKS = D // COLS
ONCE = 3
DIRECT = CHUNKS - ONCE
HALF = GROUP // 2
SHARE = 128
ROW_TILE = 384
SLOTS = 3


def dot(a, b):
    return jnp.dot(a, b, preferred_element_type=F32)


def silu_mul(gate, up):
    return gate / (1.0 + jnp.exp(-gate)) * up


def count(shape, dim):
    return lax.broadcasted_iota(jnp.int32, shape, dim).astype(F32)


def quotient(values, by):
    return jnp.floor((values + 0.5) * (1.0 / by))


def ones_where(condition):
    return jnp.where(condition, 1.0, 0.0)


def kernel(
    tokens, ids, weights, eg, eu, ed, sg, su, sd, out,
    held, out1, in1, in2, ao, ai, ae, xo, xi, xe, acc_g, acc_u, hidden, hidden_a, wgu, wds, ws, wsd, acc_s, hid_s,
    pick, mix, pick_a, mix_a, spread, merge, square, work, meta, meta_all, slots_out, slots_in, from_sib, from_x, extra_out, extra, out_v,
    load_sem, gu_sem, wd_sem, own_sem, meta_s, meta_r, sm_s, sm_r, ag_s, ag_r, fw_s, fw_r, own_s, own_r,
    d_s, d_r, c_s, c_r, ad_s, ad_r, ac_s, ac_r, xd_s, xd_r, xc_s, xc_r, rs_s, rs_r, rx_s, rx_r, ex_s, ex_r, out_sem,
):
    node = lax.axis_index("node")
    local = lax.axis_index("local")
    z, y, x, core = node // 4, node % 4, local // 2, local % 2
    sib = (node, 2 * x + (1 - core))

    def far(j):
        return ((z + j // 4) % 4) * 4 + (y + j % 4) % 4

    def side(k):
        return (node, 2 * ((x + k) % 4) + core)

    def mate(k):
        return (local + k) % LOCALS

    def block(i, size):
        return pl.ds(pl.multiple_of(i * size, size), size)

    def by_tiles(rows, work_on):
        @pl.loop(0, rows // ROW_TILE)
        def _(i):
            work_on(block(i, ROW_TILE))

    def columns(c):
        return block(c, COLS)

    def tok_rows(i):
        return block(i, TOK)

    def remote(src, dst, send, recv, device):
        return pltpu.make_async_remote_copy(
            src_ref=src, dst_ref=dst, send_sem=send, recv_sem=recv, device_id=device, device_id_type=MESH
        )

    def settled(ref, sem):
        pltpu.make_async_copy(ref, ref, sem).wait()

    barrier = pltpu.get_barrier_semaphore()
    for j in range(1, NODES):
        pl.semaphore_signal(barrier, inc=1, device_id=(far(j), local), device_id_type=MESH)
    for k in range(1, LOCALS):
        pl.semaphore_signal(barrier, inc=1, device_id=(node, mate(k)), device_id_type=MESH)

    loads = [
        pltpu.make_async_copy(sg, ws.at[:, pl.ds(0, SHARE)], load_sem.at[0]),
        pltpu.make_async_copy(su, ws.at[:, pl.ds(SHARE, SHARE)], load_sem.at[1]),
        pltpu.make_async_copy(sd, wsd, load_sem.at[2]),
    ]

    def own_copy(c):
        return pltpu.make_async_copy(tokens.at[:, columns(c)], held.at[c, core, tok_rows(x)], own_sem.at[c])

    def gate_load(c, s):
        return pltpu.make_async_copy(eg.at[0, columns(c)], wgu.at[s, 0], gu_sem.at[s, 0])

    def up_load(c, s):
        return pltpu.make_async_copy(eu.at[0, columns(c)], wgu.at[s, 1], gu_sem.at[s, 1])

    def down_load(c, s):
        return pltpu.make_async_copy(ed.at[0, :, columns(c)], wds.at[s], wd_sem.at[s])

    def in_turn(q):
        return (1 - q % 2) * ONCE + q // 2

    for c in range(CHUNKS):
        own_copy(c).start()

    meta[...] = jnp.zeros_like(meta)
    meta[0:TOP, 0:TOK] = ids[...].astype(F32) + 1.0
    meta[TOP : 2 * TOP, 0:TOK] = weights[...].astype(F32)

    pl.semaphore_wait(barrier, NODES - 1 + LOCALS - 1)

    def meta_copy(k, s):
        return remote(meta, meta_all.at[core * 4 + x], meta_s.at[s], meta_r.at[s], (node, mate(k)))

    def gather_copy(c, k):
        return remote(tokens.at[:, columns(c)], held.at[c, core, tok_rows(x)], ag_s.at[c], ag_r.at[c], side(k))

    def forward_copy(c, k):
        mid = held.at[c, core, tok_rows((x + 4 - k) % 4)]
        if k == 0:
            return remote(tokens.at[:, columns(c)], mid, own_s.at[c], own_r.at[c], sib)
        return remote(mid, mid, fw_s.at[c], fw_r.at[c], sib)

    def three_wait(sem, c):
        settled(held.at[c, 0, pl.ds(0, 3 * TOK)], sem.at[c])

    to_sib = 1 + 6 * core
    meta_copy(to_sib, 0).start()
    for c in range(CHUNKS):
        forward_copy(c, 0).start()
    for k in range(2, LOCALS - 1):
        meta_copy(k, 1).start()
    meta_copy(LOCALS - to_sib, 1).start()

    @pl.loop(0, CHUNKS)
    def _(i):
        for k in (1, 3, 2):
            gather_copy((i + ONCE) % CHUNKS, k).start()

    meta_all[core * 4 + x] = meta[...]
    meta_copy(to_sib, 0).wait_recv()

    chip_table = jnp.concatenate([meta_all[x][:, :TOK], meta_all[4 + x][:, :TOK]], axis=1)
    chip_node = quotient(chip_table[:TOP] - 1.0, LOCALS)
    node_row = count((NODES, PAIR), 0)
    chosen = jnp.zeros((NODES, PAIR), F32)
    for k in range(0, TOP, 2):
        chosen = chosen + ones_where(chip_node[k : k + 1] == node_row)
    earlier = count((PAIR, PAIR), 0) < count((PAIR, PAIR), 1)
    rank_a = dot(chosen.astype(BF16), ones_where(earlier).astype(BF16))
    rank_a = jnp.where(chosen > 0.5, rank_a, -1.0)
    place_a = count((SLOT, PAIR), 0)
    for n in range(NODES):
        pick_a[n * SLOT : (n + 1) * SLOT] = ones_where(rank_a[n : n + 1] == place_a).astype(BF16)

    def notes_copy(j):
        there = far(j)
        return remote(slots_out.at[there], slots_in.at[node], sm_s.at[0], sm_r.at[0], (there, local))

    def rows_copy(src, dst, send, recv, c, j):
        there = far(j)
        return remote(
            src.at[c, block(there, SLOT)], dst.at[c, block(node, SLOT)], send.at[c], recv.at[c], (there, local)
        )

    def rows_wait(ref, sem, c):
        settled(ref.at[c, pl.ds(0, (NODES - 1) * SLOT)], sem.at[c])

    def lanes_wait(ref, sem, a):
        settled(ref.at[a, pl.ds(0, (LOCALS - 1) * BAND)], sem.at[a])

    mine = block(node, SLOT)
    wide = block(core, WIDE)

    def once_rows(a):
        own_copy(a).wait()
        forward_copy(a, 0).wait_recv()
        rows = jnp.concatenate([held[a, 0, tok_rows(x), wide], held[a, 1, tok_rows(x), wide]], axis=0)
        ao[a] = dot(pick_a[...], rows).astype(BF16)
        for j in range(1, NODES):
            rows_copy(ao, ai, ad_s, ad_r, a, j).start()
        ai[a, mine] = ao[a, mine]

    once_rows(0)

    slots_out[...] = jnp.zeros_like(slots_out)
    notes = lax.dot_general(
        chip_table.astype(BF16), pick_a[...], (((1,), (1,)), ((), ())), preferred_element_type=F32
    )
    for n in range(NODES):
        slots_out[n, :, 0:SLOT] = notes[:, n * SLOT : (n + 1) * SLOT]

    for j in range(1, NODES):
        notes_copy(j).start()
    slots_in[node] = slots_out[node]

    @pl.loop(1, ONCE)
    def _(a):
        once_rows(a)

    for load in loads:
        load.start()
    for s in range(SLOTS):
        gate_load(in_turn(s), s).start()
        up_load(in_turn(s), s).start()
    for s, c in enumerate((ONCE, 0, 1)):
        down_load(c, s).start()

    def hand_on(c):
        three_wait(ag_r, c)
        for k in (1, 3, 2):
            forward_copy(c, k).start()

    def gathered(c):
        three_wait(fw_r, c)

    def shared_add(c):
        @pl.loop(0, 2)
        def _(h):
            acc_s[block(h, HALF)] += dot(held[c, h], ws[columns(c), :])

    def direct_rows(b):
        c = b + ONCE
        own_copy(c).wait()
        forward_copy(c, 0).wait_recv()
        hand_on(c)
        gathered(c)

        def select(tile):
            out1[b, tile] = dot(pick[tile], held[c].reshape(GROUP, COLS)).astype(BF16)

        by_tiles(ROWS, select)
        for j in range(1, NODES):
            rows_copy(out1, in1, d_s, d_r, b, j).start()
        in1[b, mine] = out1[b, mine]
        shared_add(c)

    def pass_copy(a, k):
        there = mate(k)
        return remote(
            xo.at[a, block(there, BAND)], xi.at[a, block(core * 4 + x, BAND)], xd_s.at[a], xd_r.at[a], (node, there)
        )

    def pass_rows(a):
        rows_wait(ai, ad_r, a)

        def select(tile):
            xo[a, tile] = dot(spread[tile], ai[a]).astype(BF16)

        by_tiles(SPREAD, select)
        for k in range(1, LOCALS):
            pass_copy(a, k).start()
        xi[a, block(core * 4 + x, BAND)] = xo[a, block(local, BAND)]

    first, then = count((ROWS, 1), 0), count((1, ROWS), 1)
    earlier = (first < then) & (quotient(first, SLOT) == quotient(then, SLOT))
    square[...] = ones_where(earlier).astype(BF16)

    settled(slots_in.at[pl.ds(0, NODES - 1)], sm_s.at[0])
    settled(slots_in.at[pl.ds(0, NODES - 1)], sm_r.at[0])
    slot_table = jnp.concatenate([slots_in[n][:, :SLOT] for n in range(NODES)], axis=1)
    expert = count((LOCALS, ROWS), 0) + (node * LOCALS + 1).astype(F32)
    chosen = jnp.zeros((LOCALS, ROWS), F32)
    gain_a = jnp.zeros((LOCALS, ROWS), F32)
    for k in range(TOP):
        hit = ones_where(slot_table[k : k + 1] == expert)
        chosen = chosen + hit
        gain_a = gain_a + hit * slot_table[TOP + k : TOP + k + 1]
    slot_row = count((1, ROWS), 1)
    seat = dot(chosen.astype(BF16), square[...]) + quotient(slot_row, SLOT) * PART
    seat = jnp.where(chosen > 0.5, seat, -1.0)
    place_x = count((BAND, ROWS), 0)
    for l in range(LOCALS):
        spread[l * BAND : (l + 1) * BAND] = ones_where(seat[l : l + 1] == place_x).astype(BF16)

    meta_copy(to_sib, 0).wait_send()
    settled(meta_all.at[pl.ds(0, LOCALS - 2)], meta_s.at[1])
    settled(meta_all.at[pl.ds(0, LOCALS - 2)], meta_r.at[1])

    table = jnp.concatenate([meta_all[d][:, :TOK] for d in range(LOCALS)], axis=1)
    expert = count((NODES, GROUP), 0) * LOCALS + (local + 1).astype(F32)
    chosen = jnp.zeros((NODES, GROUP), F32)
    gain = jnp.zeros((NODES, GROUP), F32)
    for k in range(TOP):
        hit = ones_where(table[k : k + 1] == expert)
        chosen = chosen + hit
        gain = gain + hit * table[TOP + k : TOP + k + 1]

    def chip_of(t):
        device = quotient(t, TOK)
        return device - 4.0 * quotient(device, 4)

    first, then = count((GROUP, 1), 0), count((1, GROUP), 1)
    earlier = (first < then) & (chip_of(first) == chip_of(then))
    rank = dot(chosen.astype(BF16), ones_where(earlier).astype(BF16)) + chip_of(then) * PART
    rank = jnp.where(chosen > 0.5, rank, -1.0)
    place = count((SLOT, GROUP), 0)
    for n in range(NODES):
        pick[n * SLOT : (n + 1) * SLOT] = ones_where(rank[n : n + 1] == place).astype(BF16)

    acc_s[...] = jnp.zeros_like(acc_s)
    loads[0].wait()
    loads[1].wait()

    @pl.loop(0, DIRECT)
    def _(b):
        @pl.when(b < ONCE)
        def _():
            pass_rows(b)

        direct_rows(b)

    @pl.loop(0, ONCE)
    def _(a):
        hand_on(a)

    @pl.loop(0, ONCE)
    def _(a):
        gathered(a)
        shared_add(a)

    hid_s[...] = silu_mul(acc_s[:, :SHARE], acc_s[:, SHARE:]).astype(BF16)
    loads[2].wait()

    def sib_copy(c):
        return remote(held.at[c, 1 - core], from_sib.at[c], rs_s.at[c], rs_r.at[c], sib)

    def reduce_copy(c, k):
        return remote(
            held.at[c, core, tok_rows((x + k) % 4)], from_x.at[c, k], rx_s.at[c], rx_r.at[c], side(k)
        )

    def extra_copy(a):
        return remote(extra_out.at[a], extra.at[a, core], ex_s.at[a], ex_r.at[a], sib)

    def gather_sent(c):
        three_wait(ag_s, c)
        three_wait(fw_s, c)
        forward_copy(c, 0).wait_send()

    def shared_part(c, h):
        return dot(hid_s[block(h, HALF)], wsd[:, columns(c)])

    def reduce(c):
        sib_copy(c).start()
        sib_copy(c).wait_recv()
        held[c, core] = (held[c, core].astype(F32) + from_sib[c].astype(F32)).astype(BF16)
        for k in (1, 3, 2):
            reduce_copy(c, k).start()

    def reduced(c):
        total = held[c, core, tok_rows(x)].astype(F32)
        settled(from_x.at[c, pl.ds(1, 3)], rx_r.at[c])
        for k in (1, 3, 2):
            total = total + from_x[c, k].astype(F32)
        return total

    def out_copy(c):
        return pltpu.make_async_copy(out_v.at[c], out.at[:, columns(c)], out_sem.at[c])

    def finish(c):
        out_v[c] = reduced(c).astype(BF16)
        out_copy(c).start()

    def finish_once(a):
        total = reduced(a)
        rows_wait(ae, ac_r, a)
        sums = dot(mix_a[...], ae[a])
        extra_out[a] = jnp.where(core == 0, sums[TOK:], sums[:TOK])
        extra_copy(a).start()
        extra[a, core] = jnp.where(core == 0, sums[:TOK], sums[TOK:])
        extra_copy(a).wait_recv()
        out_v[a] = (total + jnp.concatenate([extra[a, 0], extra[a, 1]], axis=1)).astype(BF16)
        out_copy(a).start()

    def direct_sums(b):
        rows_wait(in2, c_r, b)
        c = b + ONCE
        gather_sent(c)

        @pl.loop(0, 2)
        def _(h):
            held[c, h] = (dot(mix[block(h, HALF)], in2[b]) + shared_part(c, h)).astype(BF16)

        reduce(c)

    @pl.loop(0, ONCE)
    def _(a):
        gather_sent(a)

        @pl.loop(0, 2)
        def _(h):
            held[a, h] = shared_part(a, h).astype(BF16)

        reduce(a)

    def clear(tile):
        acc_g[tile] = jnp.zeros((ROW_TILE, H), F32)
        acc_u[tile] = jnp.zeros((ROW_TILE, H), F32)

    by_tiles(ROWS, clear)

    row, column = count((ROWS, 1), 0), count((1, ROWS), 1)
    by_node = quotient(row, SLOT)
    by_chip = quotient(row - by_node * SLOT, PART)
    square[...] = ones_where(row - by_node * SLOT - by_chip * PART + by_chip * BAND + by_node * PART == column).astype(BF16)
    for n in range(NODES):
        hit = jnp.where(rank[n : n + 1] == place, gain[n : n + 1], 0.0)
        mix[:, n * SLOT : (n + 1) * SLOT] = jnp.transpose(hit).astype(BF16)
    for n in range(0, NODES, 8):
        hits = [ones_where(rank_a[i : i + 1] == place_a) for i in range(n, n + 8)]
        mix_a[:, n * SLOT : (n + 8) * SLOT] = jnp.transpose(jnp.concatenate(hits, axis=0)).astype(BF16)
    for l in range(0, LOCALS, 2):
        hits = [jnp.where(seat[i : i + 1] == place_x, gain_a[i : i + 1], 0.0) for i in (l, l + 1)]
        merge[:, l * BAND : (l + 2) * BAND] = jnp.transpose(jnp.concatenate(hits, axis=0)).astype(BF16)

    def gate_up(q, get):
        s = q % SLOTS
        gate_load(0, s).wait()
        up_load(0, s).wait()

        def add(tile):
            rows = get(tile)
            acc_g[tile] += dot(rows, wgu[s, 0])
            acc_u[tile] += dot(rows, wgu[s, 1])

        by_tiles(ROWS, add)

        @pl.when(q + SLOTS < CHUNKS)
        def _():
            gate_load(in_turn(q + SLOTS), s).start()
            up_load(in_turn(q + SLOTS), s).start()

    @pl.loop(0, ONCE)
    def _(i):
        rows_wait(in1, d_r, i)
        gate_up(2 * i, lambda tile: in1[i, tile])
        lanes_wait(xi, xd_r, i)

        def reorder(tile):
            for h in range(2):
                work[tile, h * WIDE : (h + 1) * WIDE] = dot(square[tile], xi[i, h * ROWS : (h + 1) * ROWS]).astype(BF16)

        by_tiles(ROWS, reorder)
        gate_up(2 * i + 1, lambda tile: work[tile])

    by_chip = quotient(row, BAND)
    by_node = quotient(row - by_chip * BAND, PART)
    square[...] = ones_where(row - by_chip * BAND - by_node * PART + by_node * SLOT + by_chip * PART == column).astype(BF16)

    rows_wait(out1, d_s, 0)
    down_load(0, 0).wait()
    last = DIRECT - 1
    s_last = (CHUNKS - 1) % SLOTS
    gate_load(0, s_last).wait()
    up_load(0, s_last).wait()
    rows_wait(in1, d_r, last)

    @pl.loop(0, 4)
    def _(t):
        tile = block(t, BAND)
        rows = in1[last, tile]
        gate = acc_g[tile] + dot(rows, wgu[s_last, 0])
        up = acc_u[tile] + dot(rows, wgu[s_last, 1])
        hidden[tile] = silu_mul(gate, up).astype(BF16)
        out1[0, tile] = dot(hidden[tile], wds[0]).astype(BF16)
        for n in range(4):
            j = (t + 4 - z) % 4 * 4 + (n + 4 - y) % 4

            @pl.when(j != 0)
            def _():
                rows_copy(out1, in2, c_s, c_r, 0, j).start()

    in2[0, mine] = out1[0, mine]
    down_load(2, 0).start()

    def reorder_hidden(tile):
        hidden_a[tile] = dot(square[tile], hidden[...]).astype(BF16)

    by_tiles(ROWS, reorder_hidden)

    def back_copy(a, k):
        there = mate(k)
        return remote(
            xo.at[a, block(there % 2 * 4 + there // 2, BAND)], xe.at[a, block(local, BAND)],
            xc_s.at[a], xc_r.at[a], (node, there),
        )

    @pl.loop(0, ONCE)
    def _(a):
        lanes_wait(xo, xd_s, a)
        s = (a + 1) % SLOTS
        down_load(0, s).wait()

        @pl.loop(0, ROWS // ROW_TILE)
        def _(i):
            for h in range(2):
                part = dot(hidden_a[block(i, ROW_TILE)], wds[s, :, h * WIDE : (h + 1) * WIDE])
                xo[a, block(h * (ROWS // ROW_TILE) + i, ROW_TILE)] = part.astype(BF16)

        down_load(a + 4, s).start()
        for k in range(1, LOCALS):
            back_copy(a, k).start()
        xe[a, block(local, BAND)] = xo[a, block(core * 4 + x, BAND)]

    def node_sums(a):
        rows_wait(ao, ad_s, a)
        lanes_wait(xe, xc_r, a)

        def add(tile):
            ao[a, tile] = dot(merge[tile], xe[a]).astype(BF16)

        by_tiles(ROWS, add)
        for j in range(1, NODES):
            rows_copy(ao, ae, ac_s, ac_r, a, j).start()
        ae[a, mine] = ao[a, mine]

    def direct_back(b):
        rows_wait(out1, d_s, b)
        s = b % SLOTS
        down_load(0, s).wait()

        def down(tile):
            out1[b, tile] = dot(hidden[tile], wds[s]).astype(BF16)

        by_tiles(ROWS, down)
        for j in range(1, NODES):
            rows_copy(out1, in2, c_s, c_r, b, j).start()
        in2[b, mine] = out1[b, mine]

    @pl.loop(1, DIRECT)
    def _(b):
        @pl.when(b > 1)
        def _():
            node_sums(b - 2)

        direct_back(b)

    @pl.loop(0, DIRECT)
    def _(b):
        @pl.when(b == 2)
        def _():
            node_sums(ONCE - 1)

        @pl.when(b >= 2)
        def _():
            finish_once(b - 2)

        direct_sums(b)

        @pl.when(b >= 1)
        def _():
            finish(ONCE + b - 1)

    finish_once(ONCE - 1)
    finish(CHUNKS - 1)

    @pl.loop(0, DIRECT)
    def _(b):
        rows_wait(out1, c_s, b)

    @pl.loop(0, ONCE)
    def _(a):
        lanes_wait(xo, xc_s, a)
        rows_wait(ao, ac_s, a)
        extra_copy(a).wait_send()

    @pl.loop(0, CHUNKS)
    def _(c):
        sib_copy(c).wait_send()
        settled(from_x.at[c, pl.ds(1, 3)], rx_s.at[c])
        out_copy(c).wait()


def on_device(tokens, ids, weights, *matrices):
    vmem = pl.BlockSpec(memory_space=pltpu.VMEM)
    hbm = pl.BlockSpec(memory_space=pl.ANY)
    dma = pltpu.SemaphoreType.DMA
    return pl.pallas_call(
        kernel,
        out_shape=jax.ShapeDtypeStruct((TOK, D), BF16),
        in_specs=[hbm, vmem, vmem] + [hbm] * 6,
        out_specs=hbm,
        scratch_shapes=[
            pltpu.VMEM((CHUNKS, 2, HALF, COLS), BF16),
            pltpu.VMEM((DIRECT, ROWS, COLS), BF16),
            pltpu.VMEM((DIRECT, ROWS, COLS), BF16),
            pltpu.VMEM((DIRECT, ROWS, COLS), BF16),
            pltpu.VMEM((ONCE, ROWS, WIDE), BF16),
            pltpu.VMEM((ONCE, ROWS, WIDE), BF16),
            pltpu.VMEM((ONCE, ROWS, WIDE), BF16),
            pltpu.VMEM((ONCE, SPREAD, WIDE), BF16),
            pltpu.VMEM((ONCE, SPREAD, WIDE), BF16),
            pltpu.VMEM((ONCE, SPREAD, WIDE), BF16),
            pltpu.VMEM((ROWS, H), F32),
            pltpu.VMEM((ROWS, H), F32),
            pltpu.VMEM((ROWS, H), BF16),
            pltpu.VMEM((ROWS, H), BF16),
            pltpu.VMEM((SLOTS, 2, COLS, H), BF16),
            pltpu.VMEM((SLOTS, H, COLS), BF16),
            pltpu.VMEM((D, 2 * SHARE), BF16),
            pltpu.VMEM((SHARE, D), BF16),
            pltpu.VMEM((GROUP, 2 * SHARE), F32),
            pltpu.VMEM((GROUP, SHARE), BF16),
            pltpu.VMEM((ROWS, GROUP), BF16),
            pltpu.VMEM((GROUP, ROWS), BF16),
            pltpu.VMEM((ROWS, PAIR), BF16),
            pltpu.VMEM((PAIR, ROWS), BF16),
            pltpu.VMEM((SPREAD, ROWS), BF16),
            pltpu.VMEM((ROWS, SPREAD), BF16),
            pltpu.VMEM((ROWS, ROWS), BF16),
            pltpu.VMEM((ROWS, COLS), BF16),
            pltpu.VMEM((2 * TOP, 128), F32),
            pltpu.VMEM((LOCALS, 2 * TOP, 128), F32),
            pltpu.VMEM((NODES, 2 * TOP, 128), F32),
            pltpu.VMEM((NODES, 2 * TOP, 128), F32),
            pltpu.VMEM((CHUNKS, HALF, COLS), BF16),
            pltpu.VMEM((CHUNKS, 4, TOK, COLS), BF16),
            pltpu.VMEM((ONCE, TOK, WIDE), F32),
            pltpu.VMEM((ONCE, 2, TOK, WIDE), F32),
            pltpu.VMEM((CHUNKS, TOK, COLS), BF16),
            dma((3,)),
            dma((SLOTS, 2)),
            dma((SLOTS,)),
            dma((CHUNKS,)),
            dma((2,)),
            dma((2,)),
            dma((1,)),
            dma((1,)),
            dma((CHUNKS,)),
            dma((CHUNKS,)),
            dma((CHUNKS,)),
            dma((CHUNKS,)),
            dma((CHUNKS,)),
            dma((CHUNKS,)),
            dma((DIRECT,)),
            dma((DIRECT,)),
            dma((DIRECT,)),
            dma((DIRECT,)),
            dma((ONCE,)),
            dma((ONCE,)),
            dma((ONCE,)),
            dma((ONCE,)),
            dma((ONCE,)),
            dma((ONCE,)),
            dma((ONCE,)),
            dma((ONCE,)),
            dma((CHUNKS,)),
            dma((CHUNKS,)),
            dma((CHUNKS,)),
            dma((CHUNKS,)),
            dma((ONCE,)),
            dma((ONCE,)),
            dma((CHUNKS,)),
        ],
        compiler_params=pltpu.CompilerParams(
            collective_id=0, has_side_effects=True, vmem_limit_bytes=63 * 2**20
        ),
        cost_estimate=pl.CostEstimate(flops=32 * 10**9, bytes_accessed=26 * 10**6, transcendentals=10**6),
        name="moe",
    )(tokens, ids.T, weights.T, *matrices)


def solution(mesh):
    both = ("node", "local")
    in_specs = (
        P(both, None),
        P(both, None),
        P(both, None),
        P(both, None, None),
        P(both, None, None),
        P(both, None, None),
        P(None, "local"),
        P(None, "local"),
        P("local", None),
    )
    return jax.shard_map(on_device, mesh=mesh, in_specs=in_specs, out_specs=P(both, None), check_vma=False)
```
